512 devices in a mesh: dom: 64 (over x, z), head: 8 (over y, core).
Axes of the slice: x: 4, y: 4, z: 16, core: 2. Of those that a mesh axis runs over, the one named last changes fastest.
Arguments:
- node_feats: bfloat16 [65536, 512], P(('dom', 'head')), may hold values from -6 to 6
- norm_gain: float32 [512], replicated, may hold values from 0.25 to 1.75
- w_qkv: bfloat16 [512, 1536], P(None, 'head'), may hold values from -1 to 1
- w_out: bfloat16 [512, 512], replicated, may hold values from -0.25 to 0.25
- rand_feat: float32 [8, 64, 256], P('head'), may hold values from -6 to 6
- temper: float32 [8], P('head'), may hold values from 1 to 6
- edge_src: int32 [512, 6], P('dom'), may hold values from 0 to 511, as said below
- edge_count: int32 [512], P('dom'), may hold values from 1 to 6, as said below
- block_fill: int32 [512], replicated, may hold values from 32 to 128, as said below
Outputs:
- update: bfloat16 [65536, 512], P(('dom', 'head'))
The draws below stay inside these ranges and needn't reach their ends.
Inputs may be any that keep to these rules, and one draw needn't show every extreme that they name: `edge_src`: destination block b lies in partition p = b // 8; each of its source blocks lies in partition p - 1, p or p + 1; slot 0 holds b itself, and slots at or beyond edge_count[b] hold b. `edge_count`: every block of some partition uses all 6 slots. `block_fill`: block 0 is full.
All inputs are finite; a program needn't handle non-finite values.
Results may differ from the reference program's by a relative error of at most 0.012.
The reference program's roundings to bfloat16 on the way (of `normed`, `qkv` and `mixed`) count: a program that leaves them out, or rounds other values in their place, can miss the bound.
Values may be sent and summed in bfloat16 or wider, within the bound.
A program may use at most 64 MiB of HBM per device.

```python
import math
import jax
import jax.numpy as jnp
from jax import lax

D = 512
H = 8
DH = 64
M = 256
BLK = 128
MAXE = 6
PART_ROWS = 1024
PBLK = 8
NODES = 65536
NBLK = 512
N_DOM = 64


def edge_tables(key):
    total_blocks = PBLK * N_DOM
    key_list = jax.random.split(jax.random.fold_in(key, 11), 5)
    block_ids = jnp.arange(total_blocks, dtype=jnp.int32)
    owner = block_ids // PBLK
    limit_part = jax.random.randint(key_list[0], (N_DOM,), 1, MAXE + 1)
    busiest = jax.random.randint(key_list[1], (), 0, N_DOM)
    limit_part = jnp.where(jnp.arange(N_DOM) == busiest, MAXE, limit_part)
    drawn_count = jax.random.randint(key_list[2], (total_blocks,), 0, MAXE)
    counts = 1 + drawn_count % limit_part[owner]
    counts = jnp.where(owner == busiest, MAXE, counts)
    side_step = jax.random.randint(key_list[3], (total_blocks, MAXE), -1, 2)
    source_part = jnp.clip(owner[:, None] + side_step, 0, N_DOM - 1)
    inner_block = jax.random.randint(key_list[4], (total_blocks, MAXE), 0, PBLK)
    sources = source_part * PBLK + inner_block
    slot_ids = jnp.arange(MAXE, dtype=jnp.int32)[None, :]
    sources = jnp.where((slot_ids == 0) | (slot_ids >= counts[:, None]), block_ids[:, None], sources)
    return (sources.astype(jnp.int32), counts.astype(jnp.int32))


def draw_edge_src(key, part):
    return edge_tables(key)[0]


def draw_edge_count(key, part):
    return edge_tables(key)[1]


def draw_block_fill(key, part):
    total_blocks = PBLK * N_DOM
    fills = jax.random.randint(jax.random.fold_in(key, 23), (total_blocks,), BLK // 4, BLK + 1)
    block_ids = jnp.arange(total_blocks, dtype=jnp.int32)
    return jnp.where(block_ids == 0, BLK, fills).astype(jnp.int32)


def planted_direction(key):
    key_list = jax.random.split(jax.random.fold_in(key, 31), 2)
    signs = jnp.where(jax.random.bernoulli(key_list[0], 0.5, (D,)), 1.0, -1.0).astype(jnp.float32)
    chosen_head = jax.random.randint(key_list[1], (), 0, H)
    return (signs, chosen_head)


def draw_w_qkv(key, part):
    signs, chosen_head = planted_direction(key)
    base = jax.random.normal(jax.random.fold_in(key, 41), (D, H * 3 * DH), jnp.float32) * D ** (-0.5)
    base = jnp.clip(base, -4.0 * D ** (-0.5), 4.0 * D ** (-0.5))
    factor = min(1.0, (D / 512.0) ** 0.5)
    columns = jnp.arange(H * 3 * DH, dtype=jnp.int32)
    column_head = columns // (3 * DH)
    column_kind = columns // DH % 3
    strength = jnp.where(column_kind == 0, 1.5, jnp.where(column_kind == 1, 21.0, 0.0)) * factor / D
    strength = jnp.where(column_head == chosen_head, strength, 0.0)
    return (base + signs[:, None] * strength[None, :]).astype(jnp.bfloat16)


def draw_node_feats(key, part):
    base = jax.random.normal(jax.random.fold_in(key, 51), (NODES, D), jnp.float32)
    return jnp.clip(base, -6.0, 6.0).astype(jnp.bfloat16)


def shard_levels(key, shape, cuts, low, top_value):
    level, own = 1.0, jax.random.fold_in(key, 6)
    for axis_at, parts in cuts:
        draws = jnp.exp(jax.random.uniform(jax.random.fold_in(own, axis_at), (parts,), jnp.float32, low / len(cuts), top_value / len(cuts)))
        level = level * jnp.repeat(draws, shape[axis_at] // parts).reshape([-1 if axis == axis_at else 1 for axis in range(len(shape))])
    return level


def normal_values(key, dims, width, reach, cuts=(), held_as=jnp.bfloat16):
    values = jax.random.normal(key, dims, jnp.float32) * width
    if len(cuts) > 0:
        values = shard_levels(key, dims, cuts, -0.22, 0.18) * values
    return jnp.clip(values, min=-reach, max=reach).astype(held_as)


def setup_inputs(seed: int = 0) -> dict:
    splits = jax.random.split(jax.random.key(seed), 10)
    node_feats = draw_node_feats(jax.random.fold_in(splits[9], 71), 0)
    norm_gain = jnp.clip(1.0 + 0.15 * jax.random.normal(splits[1], (D,), jnp.float32), 0.25, 1.75)
    w_qkv = draw_w_qkv(jax.random.fold_in(splits[9], 71), 0)
    w_out = normal_values(splits[3], (H * DH, D), (H * DH) ** -0.5, 0.25)
    rand_feat = normal_values(splits[4], (H, DH, M), 1.0, 6.0, ((0, 8),), jnp.float32)
    temper = jnp.clip(jnp.exp(math.log(6.0) - 1.7917595 * jax.random.uniform(splits[5], (H,), jnp.float32) ** shard_levels(splits[5], (H,), ((0, 8),), -0.2, 0.2)), 1.0, 6.0)
    edge_src = draw_edge_src(jax.random.fold_in(splits[9], 71), 0)
    edge_count = draw_edge_count(jax.random.fold_in(splits[9], 71), 0)
    block_fill = draw_block_fill(jax.random.fold_in(splits[9], 71), 0)
    return {"node_feats": node_feats, "norm_gain": norm_gain, "w_qkv": w_qkv, "w_out": w_out, "rand_feat": rand_feat, "temper": temper, "edge_src": edge_src, "edge_count": edge_count, "block_fill": block_fill}


def layer_norm(rows, gain):
    widened = rows.astype(jnp.float32)
    centred = widened - lax.optimization_barrier(jnp.mean(widened, axis=-1, keepdims=True))
    spread = lax.optimization_barrier(jnp.mean(centred * centred, axis=-1, keepdims=True))
    return (centred * lax.rsqrt(spread + 1e-05) * gain).astype(jnp.bfloat16)

def features(rows, directions, temper):
    scaled = rows.astype(jnp.float32) * (jnp.sqrt(temper)[None, :, None] * DH ** (-0.25))
    lifted = jnp.einsum('nhd,hdm->nhm', scaled, directions, precision=lax.Precision.HIGHEST)
    return jnp.exp(lifted - 0.5 * lax.optimization_barrier(jnp.sum(scaled * scaled, axis=-1, keepdims=True))) * M ** (-0.5)

def reference(node_feats, norm_gain, w_qkv, w_out, rand_feat, temper, edge_src, edge_count, block_fill):
    normed = layer_norm(node_feats, norm_gain).reshape(N_DOM, PART_ROWS, D)

    def project(rows_in):
        return jnp.dot(rows_in, w_qkv, preferred_element_type=jnp.float32).astype(jnp.bfloat16)
    qkv = lax.map(project, normed)
    qkv = lax.optimization_barrier(qkv).reshape(N_DOM, PART_ROWS, H, 3, DH)
    fill_ok = jnp.arange(BLK, dtype=jnp.int32)[None, :] < block_fill[:, None]
    valid = fill_ok.astype(jnp.float32).reshape(N_DOM, PART_ROWS)

    def summarize(packed):
        part_qkv, part_valid = packed
        phi_keys = features(part_qkv[:, :, 1], rand_feat, temper) * part_valid[:, None, None]
        values = part_qkv[:, :, 2].astype(jnp.float32)
        return (jnp.einsum('nhm,nhe->hme', phi_keys, values, precision=lax.Precision.HIGHEST), lax.optimization_barrier(jnp.sum(phi_keys, axis=0)))
    sums, totals = lax.map(summarize, (qkv, valid))
    kernel_sum = lax.optimization_barrier(jnp.sum(sums, axis=0))
    key_total = lax.optimization_barrier(jnp.sum(totals, axis=0))
    flat_blocks = qkv.reshape(NBLK, BLK, H, 3, DH)

    def output_part(packed):
        part_qkv, sources, counts = packed
        queries = part_qkv[:, :, 0]
        q_blocks = queries.reshape(PBLK, BLK, H, DH).astype(jnp.float32)
        picked = flat_blocks[sources]
        keys = picked[:, :, :, :, 1, :].astype(jnp.float32)
        values = picked[:, :, :, :, 2, :].astype(jnp.float32)
        scores = jnp.einsum('bqhd,bjkhd->bhqjk', q_blocks, keys) * DH ** (-0.5)
        used = jnp.arange(MAXE, dtype=jnp.int32)[None, :] < counts[:, None]
        allowed = fill_ok[sources] & used[:, :, None]
        scores = jnp.where(allowed[:, None, None, :, :], scores, -1e+30)
        row_max = lax.optimization_barrier(jnp.max(scores, axis=(3, 4), keepdims=True))
        weights = jnp.exp(scores - row_max)
        total = lax.optimization_barrier(jnp.sum(weights, axis=(3, 4)))
        rounded = lax.optimization_barrier(weights.astype(jnp.bfloat16)).astype(jnp.float32)
        local = jnp.einsum('bhqjk,bjkhd->bqhd', rounded, values) / jnp.transpose(total, (0, 2, 1))[..., None]
        local = local.reshape(PART_ROWS, H, DH)
        phi_queries = features(queries, rand_feat, temper)
        numer = jnp.einsum('nhm,hme->nhe', phi_queries, kernel_sum, precision=lax.Precision.HIGHEST)
        denom = jnp.einsum('nhm,hm->nh', phi_queries, key_total, precision=lax.Precision.HIGHEST)
        mixed = (local + numer / denom[..., None]).astype(jnp.bfloat16).reshape(PART_ROWS, H * DH)
        return jnp.dot(mixed, w_out, preferred_element_type=jnp.float32).astype(jnp.bfloat16)
    result = lax.map(output_part, (qkv, edge_src.reshape(N_DOM, PBLK, MAXE), edge_count.reshape(N_DOM, PBLK)))
    return result.reshape(NODES, D)
```

```python
import functools
import math

import jax
import jax.numpy as jnp
from jax import lax
from jax.experimental import pallas as pl
from jax.experimental.pallas import tpu as pltpu
from jax.sharding import PartitionSpec as P

BLK = 128
NX, NZ, NY = 4, 16, 4
HEADS = 2 * NY
BF16 = jnp.bfloat16
F32 = jnp.float32
MESH = pl.DeviceIdType.MESH
NT = (((1,), (1,)), ((), ()))
NN = (((1,), (0,)), ((), ()))


def mul(a, b, dims=NN):
    return lax.dot_general(a, b, dims, preferred_element_type=F32)


def kernel(
    feats_hbm, gain_ref, w_hbm, wout_hbm, rand_hbm, temper_ref, edge_ref, count_ref, fill_ref,
    out_hbm,
    feats, wout, rand, rot, xg, wt, kv, qq, mkv, mq, phiq, parts, rs, xs, ag, local, mixed,
    ret, outb,
    load_sem, store_sem, x_send, x_recv, w_send, w_recv, n_send, prev_recv, next_recv,
    m_send, mk_recv, mq_recv, rs_send, rs_recv, xs_send, xs_recv, ag_send, ag_recv,
    a_send, a_recv,
):
    dom = lax.axis_index("dom")
    head = lax.axis_index("head")
    y, c = head // 2, head % 2
    x, z = dom // NZ, dom % NZ
    mate = y * 2 + (1 - c)
    n_dom = NX * NZ
    right, left = (dom + 1) % n_dom, (dom + n_dom - 1) % n_dom

    loads = [
        pltpu.make_async_copy(feats_hbm, feats, load_sem.at[0]),
        pltpu.make_async_copy(w_hbm, wt.at[0], load_sem.at[1]),
        pltpu.make_async_copy(rand_hbm, rand, load_sem.at[2]),
        pltpu.make_async_copy(wout_hbm, wout, load_sem.at[3]),
    ]
    for load in loads:
        load.start()

    barrier = pltpu.get_barrier_semaphore()
    friends = [(dom, (head + o) % HEADS) for o in range(1, HEADS)]
    friends += [(d, h) for d in (left, right) for h in (head, mate)]
    friends += [(x * NZ + (z + o) % NZ, head) for o in range(1, NZ)]
    friends += [(((x + o) % NX) * NZ + z, head) for o in range(1, NX)]
    for friend in friends:
        pl.semaphore_signal(barrier, inc=1, device_id=friend, device_id_type=MESH)

    def push(src, dst, send, recv, device):
        copy = pltpu.make_async_remote_copy(
            src_ref=src, dst_ref=dst, send_sem=send, recv_sem=recv,
            device_id=device, device_id_type=MESH,
        )
        copy.start()

    def drain(like, sem):
        pltpu.make_async_copy(like, like, sem).wait()

    loads[0].wait()
    rows = feats[...].astype(F32)
    centred = rows - jnp.mean(rows, axis=-1, keepdims=True)
    spread = jnp.mean(centred * centred, axis=-1, keepdims=True)
    xg[0] = (centred * lax.rsqrt(spread + 1e-05) * gain_ref[...]).astype(BF16)

    loads[1].wait()

    pl.semaphore_wait(barrier, len(friends))
    for o in range(1, NY):
        push(xg.at[0], xg.at[o], x_send, x_recv.at[o - 1], (dom, ((y + o) % NY) * 2 + c))
    push(wt.at[0], wt.at[1], w_send, w_recv, (dom, mate))

    loads[2].wait()
    temper = temper_ref[0]
    scaled = rand[...] * (jnp.sqrt(jnp.full((1, 256), temper, F32)) * 64 ** (-0.25))
    coarse = scaled.astype(BF16).astype(F32)
    rot[...] = jnp.concatenate([coarse, scaled - coarse], axis=0).T.astype(BF16)
    half = temper * (1.0 / 16.0)
    log_root = math.log(16.0)

    drain(wt.at[1], w_recv)
    for o in range(NY):
        if o > 0:
            drain(xg.at[o], x_recv.at[o - 1])
        r = ((y + NY - o) % NY) * 2 + c
        shard = xg[o]
        wq = [wt[i, 0:64] for i in (0, 0, 1, 1)]
        kv2 = mul(jnp.concatenate([wt[0, 64:192], wt[1, 64:192]], axis=0), shard, NT).astype(BF16)
        kv[8 + r] = kv2[0:128]
        mkv[o] = kv2[128:256]
        for d, base in ((right, 0), (left, 16)):
            sem = prev_recv if base == 0 else next_recv
            push(kv.at[8 + r], kv.at[base + r], n_send, sem, (d, head))
        push(mkv.at[o], kv.at[8 + r], m_send, mk_recv, (dom, mate))
        for d, base in ((right, 0), (left, 16)):
            sem = prev_recv if base == 0 else next_recv
            push(mkv.at[o], kv.at[base + r], n_send, sem, (d, mate))
        q2 = mul(shard, jnp.concatenate(wq, axis=0), NT).astype(BF16)
        qq[r] = q2[:, 0:128]
        mq[o] = q2[:, 128:256]
        push(mq.at[o], qq.at[r], m_send, mq_recv, (dom, mate))

    lanes = lax.broadcasted_iota(jnp.int32, (8, 128), 1)[0:1]
    ones16 = jnp.ones((16, 128), BF16)
    rotated = rot[...]

    def key_features(r):
        both = kv[8 + r]
        keys = both[0:64]
        wide = keys.astype(F32)
        norm = jnp.sum(wide * wide, axis=0, keepdims=True)
        lifted = mul(rotated, jnp.concatenate([keys, keys], axis=0))
        phi = jnp.exp(lifted - (norm * half + log_root))
        phi = jnp.where(lanes < fill_ref[dom * 8 + r], phi, 0.0).astype(BF16)
        return phi, jnp.concatenate([ones16, both[64:128]], axis=0)

    drain(kv.at[pl.ds(0, 4)], mk_recv)
    sums = jnp.zeros((80, 256), F32)
    for pair in range(4):
        one, two = key_features(2 * pair), key_features(2 * pair + 1)
        sums += mul(
            jnp.concatenate([one[1], two[1]], axis=1),
            jnp.concatenate([one[0], two[0]], axis=1),
            NT,
        )
    for piece in range(NZ):
        g, j = piece // 2, piece % 2
        parts[piece] = jnp.concatenate(
            [
                sums[16 + 8 * g : 24 + 8 * g, 128 * j : 128 * j + 128],
                sums[0:8, 128 * j : 128 * j + 128],
            ],
            axis=0,
        ).astype(BF16)
    for o in range(1, NZ):
        to = (z + o) % NZ
        push(parts.at[to], rs.at[o - 1], rs_send, rs_recv, (x * NZ + to, head))

    drain(kv.at[pl.ds(0, 4)], mq_recv)
    side = lax.broadcasted_iota(jnp.int32, (128, 128), 1) < 64
    for r in range(8):
        rows_q = qq[r]
        wide = rows_q.astype(F32)
        square = wide * wide
        top = square.astype(BF16)
        rest = (square - top.astype(F32)).astype(BF16)
        norm = mul(ones16, jnp.where(side, top, rest), NT)[0:1]
        lifted = mul(rotated, rows_q, NT)
        phiq[r] = jnp.exp(lifted - (norm * half + log_root)).astype(BF16)

    drain(rs, rs_recv)
    mine = parts[z].astype(F32)
    for o in range(NZ - 1):
        mine += rs[o].astype(F32)
    xs[0] = mine.astype(BF16)
    for o in range(1, NX):
        push(xs.at[0], xs.at[o], xs_send, xs_recv, (((x + o) % NX) * NZ + z, head))

    drain(kv.at[pl.ds(0, 8)], prev_recv)
    drain(kv.at[pl.ds(0, 8)], next_recv)

    def attend(r):
        queries = (qq[r] * 0.125)[:, 0:64]
        scores, values = [], []
        for j in range(6):
            src = edge_ref[r, j]
            block = kv[jnp.clip(src - (dom - 1) * 8, 0, 23)]
            real = jnp.where(j < count_ref[r], fill_ref[src], 0)
            scores.append(jnp.where(lanes < real, mul(queries, block[0:64]), -1e30))
            values.append(jnp.concatenate([ones16, block[64:128]], axis=0))
        top = functools.reduce(jnp.maximum, scores)
        top = jnp.max(top, axis=1, keepdims=True)
        weights = [jnp.exp(s - top).astype(BF16) for s in scores]
        total = mul(jnp.concatenate(values, axis=1), jnp.concatenate(weights, axis=1), NT)
        local[r] = total[16:80] / total[0:1]

    for r in range(4):
        attend(r)

    drain(xs.at[pl.ds(1, 3)], xs_recv)
    for o in range(1, NX):
        mine += xs[o].astype(F32)
    ag[z] = mine.astype(BF16)
    for o in range(1, NZ):
        push(ag.at[z], ag.at[z], ag_send, ag_recv, (x * NZ + (z + o) % NZ, head))

    for r in range(4, 8):
        attend(r)

    drain(ag.at[pl.ds(0, NZ - 1)], ag_recv)
    got = [ag[piece].astype(F32) for piece in range(NZ)]
    stack = [jnp.concatenate([got[0][8:16], got[1][8:16]], axis=1)] * 2
    stack += [
        jnp.concatenate([got[2 * g][0:8], got[2 * g + 1][0:8]], axis=1) for g in range(8)
    ]
    whole = jnp.concatenate(stack, axis=0).astype(BF16)

    def mix(r):
        both = mul(whole, phiq[r])
        return (local[r] + both[16:80] / both[0:1]).astype(BF16)

    ret[head] = mix(head)
    for o in range(1, HEADS):
        to = (head + o) % HEADS
        mixed[o - 1] = mix(to)
        push(mixed.at[o - 1], ret.at[head], a_send, a_recv, (dom, to))
    drain(mixed, a_recv)
    loads[3].wait()
    back = ret[...].reshape(512, 128).T
    outb[...] = mul(back, wout[...]).astype(BF16)
    store = pltpu.make_async_copy(outb, out_hbm, store_sem)
    store.start()

    drain(xg.at[pl.ds(0, 3)], x_send)
    drain(wt.at[0], w_send)
    drain(kv.at[pl.ds(0, 16)], n_send)
    drain(kv.at[pl.ds(0, 8)], m_send)
    drain(rs, rs_send)
    drain(xs.at[pl.ds(1, 3)], xs_send)
    drain(rs, ag_send)
    drain(mixed, a_send)
    store.wait()


def shards(
    node_feats, norm_gain, w_qkv, w_out, rand_feat, temper, edge_src, edge_count, block_fill
):
    any_space = pl.BlockSpec(memory_space=pl.ANY)
    smem = pl.BlockSpec(memory_space=pltpu.SMEM)
    vmem = pl.BlockSpec(memory_space=pltpu.VMEM)
    dma = pltpu.SemaphoreType.DMA
    return pl.pallas_call(
        kernel,
        out_shape=jax.ShapeDtypeStruct(node_feats.shape, BF16),
        in_specs=[any_space, vmem, any_space, any_space, any_space, smem, smem, smem, smem],
        out_specs=any_space,
        scratch_shapes=[
            pltpu.VMEM((128, 512), BF16),
                pltpu.VMEM((512, 512), BF16),
            pltpu.VMEM((64, 256), F32),
            pltpu.VMEM((256, 128), BF16),
            pltpu.VMEM((NY, 128, 512), BF16),
            pltpu.VMEM((2, 192, 512), BF16),
            pltpu.VMEM((24, 128, 128), BF16),
            pltpu.VMEM((8, 128, 128), BF16),
            pltpu.VMEM((NY, 128, 128), BF16),
            pltpu.VMEM((NY, 128, 128), BF16),
            pltpu.VMEM((8, 256, 128), BF16),
            pltpu.VMEM((NZ, 16, 128), BF16),
            pltpu.VMEM((NZ - 1, 16, 128), BF16),
            pltpu.VMEM((NX, 16, 128), BF16),
            pltpu.VMEM((NZ, 16, 128), BF16),
            pltpu.VMEM((8, 64, 128), F32),
            pltpu.VMEM((HEADS - 1, 64, 128), BF16),
            pltpu.VMEM((HEADS, 64, 128), BF16),
            pltpu.VMEM((128, 512), BF16),
            dma((4,)), dma,
            dma, dma((NY - 1,)),
            dma, dma,
            dma, dma, dma,
            dma, dma, dma,
            dma, dma, dma, dma, dma, dma, dma, dma,
        ],
        compiler_params=pltpu.CompilerParams(
            collective_id=0, has_side_effects=True, vmem_limit_bytes=56 * 2**20
        ),
        name="graph_layer",
    )(
        node_feats, norm_gain.reshape(1, -1), w_qkv.T, w_out, rand_feat[0], temper, edge_src,
        edge_count, block_fill,
    )


def solution(mesh):
    return jax.shard_map(
        shards,
        mesh=mesh,
        in_specs=(
            P(("dom", "head"), None),
            P(),
            P(None, "head"),
            P(),
            P("head", None, None),
            P("head"),
            P("dom", None),
            P("dom"),
            P(),
        ),
        out_specs=P(("dom", "head"), None),
        check_vma=False,
    )
```

```python
import functools
import math

import jax
import jax.numpy as jnp
from jax import lax
from jax.experimental import pallas as pl
from jax.experimental.pallas import tpu as pltpu
from jax.sharding import PartitionSpec as P

BLK = 128
NX, NZ, NY = 4, 16, 4
QUAD = 4
CUBE = NX * QUAD
HEADS = 2 * NY
BF16 = jnp.bfloat16
F32 = jnp.float32
MESH = pl.DeviceIdType.MESH
NT = (((1,), (1,)), ((), ()))
NN = (((1,), (0,)), ((), ()))


def mul(a, b, dims=NN):
    return lax.dot_general(a, b, dims, preferred_element_type=F32)


def kernel(
    feats_hbm, gain_ref, w_hbm, wout_hbm, rand_hbm, temper_ref, edge_ref, count_ref, fill_ref,
    out_hbm,
    feats, wout, rand, rot, xg, wt, kv, qq, mkv, mq, phiq, parts, rs, xs, ag, local, mixed,
    ret, outb,
    load_sem, store_sem, x_send, x_recv, w_send, w_recv, n_send, prev_recv, next_recv,
    m_send, mk_recv, mq_recv, rs_send, rs_recv, xs_send, xs_recv, ag_send, ag_recv,
    a_send, a_recv,
):
    dom = lax.axis_index("dom")
    head = lax.axis_index("head")
    y, c = head // 2, head % 2
    x, z = dom // NZ, dom % NZ
    mate = y * 2 + (1 - c)
    n_dom = NX * NZ
    right, left = (dom + 1) % n_dom, (dom + n_dom - 1) % n_dom

    loads = [
        pltpu.make_async_copy(feats_hbm, feats, load_sem.at[0]),
        pltpu.make_async_copy(w_hbm, wt.at[0], load_sem.at[1]),
        pltpu.make_async_copy(rand_hbm, rand, load_sem.at[2]),
        pltpu.make_async_copy(wout_hbm, wout, load_sem.at[3]),
    ]
    for load in loads:
        load.start()

    barrier = pltpu.get_barrier_semaphore()
    friends = [(dom, (head + o) % HEADS) for o in range(1, HEADS)]
    friends += [(d, h) for d in (left, right) for h in (head, mate)]
    quad, low = z // QUAD, z % QUAD
    place = x * QUAD + low
    near = []
    for i in range(NX):
        for j in range(QUAD):
            if i or j:
                nx, nlow = (x + i) % NX, (low + j) % QUAD
                near.append((nx * QUAD + nlow, (nx * NZ + quad * QUAD + nlow, head)))
    far = [(x * NZ + (z + QUAD * o) % NZ, head) for o in (2, 1, 3)]
    friends += [device for _, device in near] + far
    for friend in friends:
        pl.semaphore_signal(barrier, inc=1, device_id=friend, device_id_type=MESH)

    def push(src, dst, send, recv, device):
        copy = pltpu.make_async_remote_copy(
            src_ref=src, dst_ref=dst, send_sem=send, recv_sem=recv,
            device_id=device, device_id_type=MESH,
        )
        copy.start()

    def drain(like, sem):
        pltpu.make_async_copy(like, like, sem).wait()

    loads[0].wait()
    rows = feats[...].astype(F32)
    centred = rows - jnp.mean(rows, axis=-1, keepdims=True)
    spread = jnp.mean(centred * centred, axis=-1, keepdims=True)
    xg[0] = (centred * lax.rsqrt(spread + 1e-05) * gain_ref[...]).astype(BF16)

    loads[1].wait()

    pl.semaphore_wait(barrier, len(friends))
    for o in range(1, NY):
        push(xg.at[0], xg.at[o], x_send, x_recv.at[o - 1], (dom, ((y + o) % NY) * 2 + c))
    push(wt.at[0], wt.at[1], w_send, w_recv, (dom, mate))

    loads[2].wait()
    temper = temper_ref[0]
    scaled = rand[...] * (jnp.sqrt(jnp.full((1, 256), temper, F32)) * 64 ** (-0.25))
    coarse = scaled.astype(BF16).astype(F32)
    rot[...] = jnp.concatenate([coarse, scaled - coarse], axis=0).T.astype(BF16)
    half = temper * (1.0 / 16.0)
    log_root = math.log(16.0)

    lanes = lax.broadcasted_iota(jnp.int32, (8, 128), 1)[0:1]
    ones16 = jnp.ones((16, 128), BF16)
    rotated = rot[...]

    def key_features(r):
        both = kv[8 + r]
        keys = both[0:64]
        wide = keys.astype(F32)
        norm = jnp.sum(wide * wide, axis=0, keepdims=True)
        lifted = mul(rotated, jnp.concatenate([keys, keys], axis=0))
        phi = jnp.exp(lifted - (norm * half + log_root))
        phi = jnp.where(lanes < fill_ref[dom * 8 + r], phi, 0.0).astype(BF16)
        return phi, jnp.concatenate([ones16, both[64:128]], axis=0)

    def pair_sums(o):
        drain(mkv.at[o], mk_recv.at[o])
        first = ((y + NY - o) % NY) * 2
        one, two = key_features(first), key_features(first + 1)
        return mul(
            jnp.concatenate([one[1], two[1]], axis=1),
            jnp.concatenate([one[0], two[0]], axis=1),
            NT,
        )

    drain(wt.at[1], w_recv)
    order = (0, 1, 3, 2)
    sums = jnp.zeros((80, 256), F32)
    for n, o in enumerate(order):
        if o > 0:
            drain(xg.at[o], x_recv.at[o - 1])
        r = ((y + NY - o) % NY) * 2 + c
        wkv = jnp.concatenate([wt[0, 64:192], wt[1, 64:192]], axis=0)
        kv2 = mul(wkv, xg[o], NT).astype(BF16)
        mkv[o] = kv2[128:256]
        push(mkv.at[o], kv.at[8 + r], m_send, mk_recv.at[o], (dom, mate))
        kv[8 + r] = kv2[0:128]
        for d, base, sem in ((right, 0, prev_recv), (left, 16, next_recv)):
            push(kv.at[8 + r], kv.at[base + r], n_send, sem, (d, head))
            push(mkv.at[o], kv.at[base + r], n_send, sem, (d, mate))
        if n > 0:
            sums += pair_sums(order[n - 1])
    sums += pair_sums(order[-1])
    for piece in range(CUBE):
        g, j = piece // 2, piece % 2
        parts[piece] = jnp.concatenate(
            [
                sums[16 + 8 * g : 24 + 8 * g, 128 * j : 128 * j + 128],
                sums[0:8, 128 * j : 128 * j + 128],
            ],
            axis=0,
        ).astype(BF16)
    for slot, (to, device) in enumerate(near):
        push(parts.at[to], rs.at[slot], rs_send, rs_recv, device)

    wq = jnp.concatenate([wt[i, 0:64] for i in (0, 0, 1, 1)], axis=0)
    for o in order:
        r = ((y + NY - o) % NY) * 2 + c
        q2 = mul(xg[o], wq, NT).astype(BF16)
        mq[o] = q2[:, 128:256]
        push(mq.at[o], qq.at[r], m_send, mq_recv, (dom, mate))
        qq[r] = q2[:, 0:128]
    side = lax.broadcasted_iota(jnp.int32, (128, 128), 1) < 64

    def query_features(r):
        rows_q = qq[r]
        wide = rows_q.astype(F32)
        square = wide * wide
        top = square.astype(BF16)
        rest = (square - top.astype(F32)).astype(BF16)
        norm = mul(ones16, jnp.where(side, top, rest), NT)[0:1]
        lifted = mul(rotated, rows_q, NT)
        phiq[r] = jnp.exp(lifted - (norm * half + log_root)).astype(BF16)

    for i in range(NY):
        query_features(2 * i + c)
    drain(mkv, mq_recv)
    for i in range(NY):
        query_features(2 * i + (1 - c))

    drain(rs, rs_recv)
    mine = parts[place].astype(F32)
    for o in range(CUBE - 1):
        mine += rs[o].astype(F32)
    xs[0] = mine.astype(BF16)
    for slot, device in enumerate(far):
        push(xs.at[0], xs.at[1 + slot], xs_send, xs_recv, device)

    drain(kv.at[pl.ds(0, 8)], prev_recv)
    drain(kv.at[pl.ds(0, 8)], next_recv)

    def attend(r):
        queries = (qq[r] * 0.125)[:, 0:64]
        scores, values = [], []
        for j in range(6):
            src = edge_ref[r, j]
            block = kv[jnp.clip(src - (dom - 1) * 8, 0, 23)]
            real = jnp.where(j < count_ref[r], fill_ref[src], 0)
            scores.append(jnp.where(lanes < real, mul(queries, block[0:64]), -1e30))
            values.append(jnp.concatenate([ones16, block[64:128]], axis=0))
        top = functools.reduce(jnp.maximum, scores)
        top = jnp.max(top, axis=1, keepdims=True)
        weights = [jnp.exp(s - top).astype(BF16) for s in scores]
        total = mul(jnp.concatenate(values, axis=1), jnp.concatenate(weights, axis=1), NT)
        local[r] = total[16:80] / total[0:1]

    for r in range(4):
        attend(r)

    drain(xs.at[pl.ds(1, 3)], xs_recv)
    for o in range(1, NX):
        mine += xs[o].astype(F32)
    ag[place] = mine.astype(BF16)
    for _, device in near:
        push(ag.at[place], ag.at[place], ag_send, ag_recv, device)

    for r in range(4, 8):
        attend(r)

    drain(ag.at[pl.ds(0, CUBE - 1)], ag_recv)
    got = [ag[piece].astype(F32) for piece in range(CUBE)]
    stack = [jnp.concatenate([got[0][8:16], got[1][8:16]], axis=1)] * 2
    stack += [
        jnp.concatenate([got[2 * g][0:8], got[2 * g + 1][0:8]], axis=1) for g in range(8)
    ]
    whole = jnp.concatenate(stack, axis=0).astype(BF16)

    def mix(r):
        both = mul(whole, phiq[r])
        return (local[r] + both[16:80] / both[0:1]).astype(BF16)

    ret[head] = mix(head)
    for o in range(1, HEADS):
        to = (head + o) % HEADS
        mixed[o - 1] = mix(to)
        push(mixed.at[o - 1], ret.at[head], a_send, a_recv, (dom, to))
    drain(mixed, a_recv)
    loads[3].wait()
    back = ret[...].reshape(512, 128).T
    outb[...] = mul(back, wout[...]).astype(BF16)
    store = pltpu.make_async_copy(outb, out_hbm, store_sem)
    store.start()

    drain(xg.at[pl.ds(0, 3)], x_send)
    drain(wt.at[0], w_send)
    drain(kv.at[pl.ds(0, 16)], n_send)
    drain(kv.at[pl.ds(0, 8)], m_send)
    drain(rs, rs_send)
    drain(xs.at[pl.ds(1, 3)], xs_send)
    drain(rs, ag_send)
    drain(mixed, a_send)
    store.wait()


def shards(
    node_feats, norm_gain, w_qkv, w_out, rand_feat, temper, edge_src, edge_count, block_fill
):
    any_space = pl.BlockSpec(memory_space=pl.ANY)
    smem = pl.BlockSpec(memory_space=pltpu.SMEM)
    vmem = pl.BlockSpec(memory_space=pltpu.VMEM)
    dma = pltpu.SemaphoreType.DMA
    return pl.pallas_call(
        kernel,
        out_shape=jax.ShapeDtypeStruct(node_feats.shape, BF16),
        in_specs=[any_space, vmem, any_space, any_space, any_space, smem, smem, smem, smem],
        out_specs=any_space,
        scratch_shapes=[
            pltpu.VMEM((128, 512), BF16),
                pltpu.VMEM((512, 512), BF16),
            pltpu.VMEM((64, 256), F32),
            pltpu.VMEM((256, 128), BF16),
            pltpu.VMEM((NY, 128, 512), BF16),
            pltpu.VMEM((2, 192, 512), BF16),
            pltpu.VMEM((24, 128, 128), BF16),
            pltpu.VMEM((8, 128, 128), BF16),
            pltpu.VMEM((NY, 128, 128), BF16),
            pltpu.VMEM((NY, 128, 128), BF16),
            pltpu.VMEM((8, 256, 128), BF16),
            pltpu.VMEM((CUBE, 16, 128), BF16),
            pltpu.VMEM((CUBE - 1, 16, 128), BF16),
            pltpu.VMEM((NX, 16, 128), BF16),
            pltpu.VMEM((CUBE, 16, 128), BF16),
            pltpu.VMEM((8, 64, 128), F32),
            pltpu.VMEM((HEADS - 1, 64, 128), BF16),
            pltpu.VMEM((HEADS, 64, 128), BF16),
            pltpu.VMEM((128, 512), BF16),
            dma((4,)), dma,
            dma, dma((NY - 1,)),
            dma, dma,
            dma, dma, dma,
            dma, dma((NY,)), dma,
            dma, dma, dma, dma, dma, dma, dma, dma,
        ],
        compiler_params=pltpu.CompilerParams(
            collective_id=0, has_side_effects=True, vmem_limit_bytes=56 * 2**20
        ),
        name="graph_layer",
    )(
        node_feats, norm_gain.reshape(1, -1), w_qkv.T, w_out, rand_feat[0], temper, edge_src,
        edge_count, block_fill,
    )


def solution(mesh):
    return jax.shard_map(
        shards,
        mesh=mesh,
        in_specs=(
            P(("dom", "head"), None),
            P(),
            P(None, "head"),
            P(),
            P("head", None, None),
            P("head"),
            P("dom", None),
            P("dom"),
            P(),
        ),
        out_specs=P(("dom", "head"), None),
        check_vma=False,
    )
```

```python
import functools
import math

import jax
import jax.numpy as jnp
from jax import lax
from jax.experimental import pallas as pl
from jax.experimental.pallas import tpu as pltpu
from jax.sharding import PartitionSpec as P

BLK = 128
NX, NZ, NY = 4, 16, 4
QUAD = 4
CUBE = NX * QUAD
HEADS = 2 * NY
BF16 = jnp.bfloat16
F32 = jnp.float32
MESH = pl.DeviceIdType.MESH
NT = (((1,), (1,)), ((), ()))
NN = (((1,), (0,)), ((), ()))


def mul(a, b, dims=NN):
    return lax.dot_general(a, b, dims, preferred_element_type=F32)


def kernel(
    feats_hbm, gain_hbm, w_hbm, rand_hbm, temper_hbm, edge_hbm, count_hbm, fill_hbm,
    ret,
    gain, temper_ref, edge_ref, count_ref, fill_ref, feats, rand, rot, xg, wt, kv, qq, mkv, mq, phiq, parts, rs, xs, ag, local, mixed,
    load_sem, x_send, x_recv, w_send, w_recv, n_send, prev_recv, next_recv,
    m_send, mk_recv, mq_recv, rs_send, rs_recv, xs_send, xs_recv, ag_send, ag_recv,
    a_send, a_recv,
):
    dom = lax.axis_index("dom")
    head = lax.axis_index("head")
    y, c = head // 2, head % 2
    x, z = dom // NZ, dom % NZ
    mate = y * 2 + (1 - c)
    n_dom = NX * NZ
    right, left = (dom + 1) % n_dom, (dom + n_dom - 1) % n_dom

    loads = [
        pltpu.make_async_copy(feats_hbm, feats, load_sem.at[0]),
        pltpu.make_async_copy(w_hbm, wt.at[0], load_sem.at[1]),
        pltpu.make_async_copy(rand_hbm, rand, load_sem.at[2]),
        pltpu.make_async_copy(gain_hbm, gain, load_sem.at[3]),
        pltpu.make_async_copy(temper_hbm, temper_ref, load_sem.at[4]),
        pltpu.make_async_copy(edge_hbm, edge_ref, load_sem.at[5]),
        pltpu.make_async_copy(count_hbm, count_ref, load_sem.at[6]),
        pltpu.make_async_copy(fill_hbm, fill_ref, load_sem.at[7]),
    ]
    barrier = pltpu.get_barrier_semaphore()
    friends = [(d, h) for d in (left, right) for h in (head, mate)]
    quad, low = z // QUAD, z % QUAD
    place = x * QUAD + low
    near = []
    for i in range(NX):
        for j in range(QUAD):
            if i or j:
                nx, nlow = (x + i) % NX, (low + j) % QUAD
                near.append((nx * QUAD + nlow, (nx * NZ + quad * QUAD + nlow, head)))
    far = [(x * NZ + (z + QUAD * o) % NZ, head) for o in (2, 1, 3)]
    friends = far + friends + [(dom, (head + o) % HEADS) for o in range(1, HEADS)] + [device for _, device in near]
    for friend in friends:
        pl.semaphore_signal(barrier, inc=1, device_id=friend, device_id_type=MESH)

    for load in loads:
        load.start()

    def push(src, dst, send, recv, device):
        copy = pltpu.make_async_remote_copy(
            src_ref=src, dst_ref=dst, send_sem=send, recv_sem=recv,
            device_id=device, device_id_type=MESH,
        )
        copy.start()

    def drain(like, sem):
        pltpu.make_async_copy(like, like, sem).wait()

    loads[0].wait()
    loads[3].wait()
    rows = feats[...].astype(F32)
    centred = rows - jnp.mean(rows, axis=-1, keepdims=True)
    spread = jnp.mean(centred * centred, axis=-1, keepdims=True)
    xg[0] = (centred * lax.rsqrt(spread + 1e-05) * gain[...]).astype(BF16)

    loads[1].wait()

    pl.semaphore_wait(barrier, len(friends))
    for o in range(1, NY):
        push(xg.at[0], xg.at[o], x_send, x_recv.at[o - 1], (dom, ((y + o) % NY) * 2 + c))
    push(wt.at[0], wt.at[1], w_send, w_recv, (dom, mate))

    loads[2].wait()
    for i in range(4, 8):
        loads[i].wait()
    temper = temper_ref[...]
    scaled = rand[...] * (jnp.sqrt(temper) * 64 ** (-0.25))
    coarse = scaled.astype(BF16).astype(F32)
    rot[...] = jnp.concatenate([coarse, scaled - coarse], axis=0).T.astype(BF16)
    half = temper * (1.0 / 16.0)
    log_root = math.log(16.0)

    lanes = lax.broadcasted_iota(jnp.int32, (8, 128), 1)[0:1]
    ones16 = jnp.ones((16, 128), BF16)
    rotated = rot[...]

    def key_features(r):
        both = kv[8 + r]
        keys = both[0:64]
        wide = keys.astype(F32)
        norm = jnp.sum(wide * wide, axis=0, keepdims=True)
        lifted = mul(rotated, jnp.concatenate([keys, keys], axis=0))
        phi = jnp.exp(lifted - (norm * half + log_root))
        phi = jnp.where(lanes < fill_ref[dom * 8 + r], phi, 0.0).astype(BF16)
        return phi, jnp.concatenate([ones16, both[64:128]], axis=0)

    def pair_sums(o):
        drain(mkv.at[o], mk_recv.at[o])
        first = ((y + NY - o) % NY) * 2
        one, two = key_features(first), key_features(first + 1)
        return mul(
            jnp.concatenate([one[1], two[1]], axis=1),
            jnp.concatenate([one[0], two[0]], axis=1),
            NT,
        )


    def share(o):
        r = ((y + NY - o) % NY) * 2 + c
        for d, base, sem in ((right, 0, prev_recv), (left, 16, next_recv)):
            push(kv.at[8 + r], kv.at[base + r], n_send, sem, (d, head))
            push(mkv.at[o], kv.at[base + r], n_send, sem, (d, mate))

    drain(wt.at[1], w_recv)
    order = (0, 1, 3, 2)
    sums = jnp.zeros((80, 256), F32)
    for n, o in enumerate(order):
        if o > 0:
            drain(xg.at[o], x_recv.at[o - 1])
        r = ((y + NY - o) % NY) * 2 + c
        wkv = jnp.concatenate([wt[0, 64:192], wt[1, 64:192]], axis=0)
        kv2 = mul(wkv, xg[o], NT).astype(BF16)
        mkv[o] = kv2[128:256]
        push(mkv.at[o], kv.at[8 + r], m_send, mk_recv.at[o], (dom, mate))
        kv[8 + r] = kv2[0:128]
        if n < 3:
            share(o)
        if n > 0:
            sums += pair_sums(order[n - 1])
    sums += pair_sums(order[-1])
    for piece in range(CUBE):
        g, j = piece // 2, piece % 2
        parts[piece] = jnp.concatenate(
            [
                sums[16 + 8 * g : 24 + 8 * g, 128 * j : 128 * j + 128],
                sums[0:8, 128 * j : 128 * j + 128],
            ],
            axis=0,
        ).astype(BF16)
    for slot, (to, device) in enumerate(near):
        push(parts.at[to], rs.at[slot], rs_send, rs_recv, device)
    share(order[-1])

    wq = jnp.concatenate([wt[i, 0:64] for i in (0, 0, 1, 1)], axis=0)
    for o in order:
        r = ((y + NY - o) % NY) * 2 + c
        q2 = mul(xg[o], wq, NT).astype(BF16)
        mq[o] = q2[:, 128:256]
        push(mq.at[o], qq.at[r], m_send, mq_recv, (dom, mate))
        qq[r] = q2[:, 0:128]
    side = lax.broadcasted_iota(jnp.int32, (128, 128), 1) < 64

    def query_features(r):
        rows_q = qq[r]
        wide = rows_q.astype(F32)
        square = wide * wide
        top = square.astype(BF16)
        rest = (square - top.astype(F32)).astype(BF16)
        norm = mul(ones16, jnp.where(side, top, rest), NT)[0:1]
        lifted = mul(rotated, rows_q, NT)
        phiq[r] = jnp.exp(lifted - (norm * half + log_root)).astype(BF16)

    for i in range(NY):
        query_features(2 * i + c)
    drain(mkv, mq_recv)
    for i in range(NY):
        query_features(2 * i + (1 - c))

    drain(rs, rs_recv)
    mine = parts[place].astype(F32)
    for o in range(CUBE - 1):
        mine += rs[o].astype(F32)
    xs[0] = mine.astype(BF16)
    for slot, device in enumerate(far):
        push(xs.at[0], xs.at[1 + slot], xs_send, xs_recv, device)

    drain(kv.at[pl.ds(0, 8)], prev_recv)
    drain(kv.at[pl.ds(0, 8)], next_recv)

    def attend(r):
        queries = (qq[r] * 0.125)[:, 0:64]
        scores, values = [], []
        for j in range(6):
            src = edge_ref[r, j]
            block = kv[jnp.clip(src - (dom - 1) * 8, 0, 23)]
            real = jnp.where(j < count_ref[r], fill_ref[src], 0)
            scores.append(jnp.where(lanes < real, mul(queries, block[0:64]), -1e30))
            values.append(jnp.concatenate([ones16, block[64:128]], axis=0))
        top = functools.reduce(jnp.maximum, scores)
        top = jnp.max(top, axis=1, keepdims=True)
        weights = [jnp.exp(s - top).astype(BF16) for s in scores]
        total = mul(jnp.concatenate(values, axis=1), jnp.concatenate(weights, axis=1), NT)
        local[r] = total[16:80] / total[0:1]

    for r in range(4):
        attend(r)

    drain(xs.at[pl.ds(1, 3)], xs_recv)
    for o in range(1, NX):
        mine += xs[o].astype(F32)
    ag[place] = mine.astype(BF16)
    for _, device in near:
        push(ag.at[place], ag.at[place], ag_send, ag_recv, device)

    for r in range(4, 8):
        attend(r)

    drain(ag.at[pl.ds(0, CUBE - 1)], ag_recv)
    got = [ag[piece].astype(F32) for piece in range(CUBE)]
    stack = [jnp.concatenate([got[0][8:16], got[1][8:16]], axis=1)] * 2
    stack += [
        jnp.concatenate([got[2 * g][0:8], got[2 * g + 1][0:8]], axis=1) for g in range(8)
    ]
    whole = jnp.concatenate(stack, axis=0).astype(BF16)

    def mix(r):
        both = mul(whole, phiq[r])
        return (local[r] + both[16:80] / both[0:1]).astype(BF16)

    for o in (4, 5, 2, 3, 6, 7, 1):
        to = head ^ o
        mixed[o - 1] = mix(to)
        push(mixed.at[o - 1], ret.at[head], a_send, a_recv, (dom, to))
    ret[head] = mix(head)
    drain(mixed, a_recv)

    drain(xg.at[pl.ds(0, 3)], x_send)
    drain(wt.at[0], w_send)
    drain(kv.at[pl.ds(0, 16)], n_send)
    drain(kv.at[pl.ds(0, 8)], m_send)
    drain(rs, rs_send)
    drain(xs.at[pl.ds(1, 3)], xs_send)
    drain(rs, ag_send)
    drain(mixed, a_send)


def shards(
    node_feats, norm_gain, w_qkv, w_out, rand_feat, temper, edge_src, edge_count, block_fill
):
    dma = pltpu.SemaphoreType.DMA
    back = pl.pallas_call(
        kernel,
        out_shape=pltpu.VMEM((HEADS, 64, 128), BF16),
        in_specs=[pl.BlockSpec(memory_space=pltpu.HBM)] * 8,
        out_specs=pl.BlockSpec(memory_space=pltpu.VMEM),
        scratch_shapes=[
            pltpu.VMEM((1, 512), F32),
            pltpu.VMEM((1, 1), F32),
            pltpu.SMEM((8, 6), jnp.int32),
            pltpu.SMEM((8,), jnp.int32),
            pltpu.SMEM((512,), jnp.int32),
            pltpu.VMEM((128, 512), BF16),
                pltpu.VMEM((64, 256), F32),
            pltpu.VMEM((256, 128), BF16),
            pltpu.VMEM((NY, 128, 512), BF16),
            pltpu.VMEM((2, 192, 512), BF16),
            pltpu.VMEM((24, 128, 128), BF16),
            pltpu.VMEM((8, 128, 128), BF16),
            pltpu.VMEM((NY, 128, 128), BF16),
            pltpu.VMEM((NY, 128, 128), BF16),
            pltpu.VMEM((8, 256, 128), BF16),
            pltpu.VMEM((CUBE, 16, 128), BF16),
            pltpu.VMEM((CUBE - 1, 16, 128), BF16),
            pltpu.VMEM((NX, 16, 128), BF16),
            pltpu.VMEM((CUBE, 16, 128), BF16),
            pltpu.VMEM((8, 64, 128), F32),
            pltpu.VMEM((HEADS - 1, 64, 128), BF16),
            dma((8,)),
            dma, dma((NY - 1,)),
            dma, dma,
            dma, dma, dma,
            dma, dma((NY,)), dma,
            dma, dma, dma, dma, dma, dma, dma, dma,
        ],
        compiler_params=pltpu.CompilerParams(
            collective_id=0, has_side_effects=True, vmem_limit_bytes=56 * 2**20
        ),
        name="graph_layer",
    )(
        node_feats, norm_gain.reshape(1, -1), w_qkv.T, rand_feat[0], temper.reshape(1, 1), edge_src,
        edge_count, block_fill,
    )
    return lax.dot_general(
        back.reshape(512, 128), w_out, (((0,), (0,)), ((), ())), preferred_element_type=F32
    ).astype(BF16)


def solution(mesh):
    return jax.shard_map(
        shards,
        mesh=mesh,
        in_specs=(
            P(("dom", "head"), None),
            P(),
            P(None, "head"),
            P(),
            P("head", None, None),
            P("head"),
            P("dom", None),
            P("dom"),
            P(),
        ),
        out_specs=P(("dom", "head"), None),
        check_vma=False,
    )
```

```python
import functools
import math

import jax
import jax.numpy as jnp
from jax import lax
from jax.experimental import pallas as pl
from jax.experimental.pallas import tpu as pltpu
from jax.sharding import PartitionSpec as P

BLK = 128
NX, NZ, NY = 4, 16, 4
QUAD = 4
CUBE = NX * QUAD
PARTS = 8
HEADS = 2 * NY
BF16 = jnp.bfloat16
F32 = jnp.float32
MESH = pl.DeviceIdType.MESH
NT = (((1,), (1,)), ((), ()))
NN = (((1,), (0,)), ((), ()))


def mul(a, b, dims=NN):
    return lax.dot_general(a, b, dims, preferred_element_type=F32)


def kernel(
    feats_hbm, gain_hbm, w_hbm, rand_hbm, temper_hbm, edge_hbm, count_hbm, fill_hbm,
    ret,
    gain, temper_ref, edge_ref, count_ref, fill_ref, feats, rand, rot, xg, wt, kv, qq, mkv, mq, phiq, parts, rs, xs, ag, tally, local, mixed,
    load_sem, x_send, x_recv, w_send, w_recv, n_send, prev_recv, next_recv,
    m_send, mk_recv, mq_recv, rs_send, rs_recv, xs_send, xs_recv, ag_send, ag_recv,
    a_send, a_recv,
):
    dom = lax.axis_index("dom")
    head = lax.axis_index("head")
    y, c = head // 2, head % 2
    x, z = dom // NZ, dom % NZ
    mate = y * 2 + (1 - c)
    n_dom = NX * NZ
    right, left = (dom + 1) % n_dom, (dom + n_dom - 1) % n_dom

    loads = [
        pltpu.make_async_copy(feats_hbm, feats, load_sem.at[0]),
        pltpu.make_async_copy(w_hbm, wt.at[0], load_sem.at[1]),
        pltpu.make_async_copy(rand_hbm, rand, load_sem.at[2]),
        pltpu.make_async_copy(gain_hbm, gain, load_sem.at[3]),
        pltpu.make_async_copy(temper_hbm, temper_ref, load_sem.at[4]),
        pltpu.make_async_copy(edge_hbm, edge_ref, load_sem.at[5]),
        pltpu.make_async_copy(count_hbm, count_ref, load_sem.at[6]),
        pltpu.make_async_copy(fill_hbm, fill_ref, load_sem.at[7]),
    ]
    barrier = pltpu.get_barrier_semaphore()
    friends = [(d, h) for d in (left, right) for h in (head, mate)]
    quad, low = z // QUAD, z % QUAD
    place = x * QUAD + low
    middle = (low + 1) // 2 == 1
    own = x * 2 + (low + 1) % 2
    near = [
        (((x + i) % NX) * NZ + quad * QUAD + (low + j) % QUAD, head)
        for i in (2, 1, 3, 0)
        for j in (3, 1, 2, 0)
        if i or j
    ]
    far = [(x * NZ + (z + QUAD * o) % NZ, head) for o in (2, 1, 3)]
    friends = far + [(dom, head ^ o) for o in (4, 5, 2, 3, 6, 7, 1)] + friends + near
    for friend in friends:
        pl.semaphore_signal(barrier, inc=1, device_id=friend, device_id_type=MESH)

    for load in loads:
        load.start()

    def push(src, dst, send, recv, device):
        copy = pltpu.make_async_remote_copy(
            src_ref=src, dst_ref=dst, send_sem=send, recv_sem=recv,
            device_id=device, device_id_type=MESH,
        )
        copy.start()

    def drain(like, sem):
        pltpu.make_async_copy(like, like, sem).wait()

    def thin(ref, i):
        return ref.at[i, pl.ds(0, 16)]

    def either(wide, ref, start, count, sem):
        @pl.when(wide)
        def _():
            drain(ref.at[pl.ds(start, count)], sem)

        @pl.when(jnp.logical_not(wide))
        def _():
            drain(ref.at[pl.ds(start, count), pl.ds(0, 16)], sem)

    def fan(ref, here, there, send, recv, device):
        @pl.when(x == 0)
        def _():
            push(ref.at[here], ref.at[there], send, recv, device)

        @pl.when(x > 0)
        def _():
            push(thin(ref, here), thin(ref, there), send, recv, device)

    loads[0].wait()
    loads[3].wait()
    rows = feats[...].astype(F32)
    centred = rows - jnp.mean(rows, axis=-1, keepdims=True)
    spread = jnp.mean(centred * centred, axis=-1, keepdims=True)
    xg[0] = (centred * lax.rsqrt(spread + 1e-05) * gain[...]).astype(BF16)

    loads[1].wait()

    pl.semaphore_wait(barrier, len(friends))
    for o in range(1, NY):
        push(xg.at[0], xg.at[o], x_send, x_recv.at[o - 1], (dom, ((y + o) % NY) * 2 + c))
    push(wt.at[0], wt.at[1], w_send, w_recv, (dom, mate))

    loads[2].wait()
    for i in range(4, 8):
        loads[i].wait()
    temper = temper_ref[...]
    scaled = rand[...] * (jnp.sqrt(temper) * 64 ** (-0.25))
    coarse = scaled.astype(BF16).astype(F32)
    rot[...] = jnp.concatenate([coarse, scaled - coarse], axis=0).T.astype(BF16)
    half = temper * (1.0 / 16.0)
    log_root = math.log(16.0)

    lanes = lax.broadcasted_iota(jnp.int32, (8, 128), 1)[0:1]
    ones16 = jnp.ones((16, 128), BF16)
    rotated = rot[...]

    def key_features(r):
        both = kv[8 + r]
        keys = both[0:64]
        wide = keys.astype(F32)
        norm = jnp.sum(wide * wide, axis=0, keepdims=True)
        lifted = mul(rotated, jnp.concatenate([keys, keys], axis=0))
        phi = jnp.exp(lifted - (norm * half + log_root))
        phi = jnp.where(lanes < fill_ref[dom * 8 + r], phi, 0.0).astype(BF16)
        return phi, jnp.concatenate([ones16, both[64:128]], axis=0)

    def pair_sums(o):
        drain(mkv.at[o], mk_recv.at[o])
        first = ((y + NY - o) % NY) * 2
        one, two = key_features(first), key_features(first + 1)
        return mul(
            jnp.concatenate([one[1], two[1]], axis=1),
            jnp.concatenate([one[0], two[0]], axis=1),
            NT,
        )


    def share(o):
        r = ((y + NY - o) % NY) * 2 + c
        for d, base, sem in ((right, 0, prev_recv), (left, 16, next_recv)):
            push(kv.at[8 + r], kv.at[base + r], n_send, sem, (d, head))
            push(mkv.at[o], kv.at[base + r], n_send, sem, (d, mate))

    drain(wt.at[1], w_recv)
    order = (0, 1, 3, 2)
    sums = jnp.zeros((80, 256), F32)
    for n, o in enumerate(order):
        if n == 3:
            sums += pair_sums(order[2])
        if o > 0:
            drain(xg.at[o], x_recv.at[o - 1])
        r = ((y + NY - o) % NY) * 2 + c
        wkv = jnp.concatenate([wt[0, 64:192], wt[1, 64:192]], axis=0)
        kv2 = mul(wkv, xg[o], NT).astype(BF16)
        mkv[o] = kv2[128:256]
        push(mkv.at[o], kv.at[8 + r], m_send, mk_recv.at[o], (dom, mate))
        kv[8 + r] = kv2[0:128]
        if n < 3:
            share(o)
        if n in (1, 2):
            sums += pair_sums(order[n - 1])
    sums += pair_sums(order[-1])
    rounded = sums.astype(BF16)
    for k in range(PARTS):
        g, columns = k // 2, slice(128 * (k % 2), 128 * (k % 2) + 128)
        parts[k, 0:16] = rounded[16 + 16 * g : 32 + 16 * g, columns]
        parts[k, 16:32] = rounded[0:16, columns]

    @pl.when(middle)
    def _():
        rs[place] = parts[own]

    for i in (2, 1, 3, 0):
        for j in (1, 2):
            to = (x + i) % NX

            @pl.when((low != j) if i == 0 else (low >= 0))
            def _():
                device = (to * NZ + quad * QUAD + j, head)
                part = to * 2 + j - 1

                @pl.when(to == 0)
                def _():
                    push(parts.at[part], rs.at[place], rs_send, rs_recv, device)

                @pl.when(to > 0)
                def _():
                    push(thin(parts, part), thin(rs, place), rs_send, rs_recv, device)

    share(order[-1])

    wq = jnp.concatenate([wt[i, 0:64] for i in (0, 0, 1, 1)], axis=0)
    for o in order:
        r = ((y + NY - o) % NY) * 2 + c
        q2 = mul(xg[o], wq, NT).astype(BF16)
        mq[o] = q2[:, 128:256]
        push(mq.at[o], qq.at[r], m_send, mq_recv, (dom, mate))
        qq[r] = q2[:, 0:128]
    side = lax.broadcasted_iota(jnp.int32, (128, 128), 1) < 64

    def query_features(r):
        rows_q = qq[r]
        wide = rows_q.astype(F32)
        square = wide * wide
        top = square.astype(BF16)
        rest = (square - top.astype(F32)).astype(BF16)
        norm = mul(ones16, jnp.where(side, top, rest), NT)[0:1]
        lifted = mul(rotated, rows_q, NT)
        phiq[r] = jnp.exp(lifted - (norm * half + log_root)).astype(BF16)

    for i in range(NY):
        query_features(2 * i + c)
    drain(mkv, mq_recv)
    for i in range(NY):
        query_features(2 * i + (1 - c))

    @pl.when(middle)
    def _():
        either(x == 0, rs, 0, CUBE - 1, rs_recv)
        xs[0] = sum(rs[i].astype(F32) for i in range(CUBE)).astype(BF16)
        for slot, device in enumerate(far):
            fan(xs, 0, 1 + slot, xs_send, xs_recv, device)

    drain(kv.at[pl.ds(0, 8)], prev_recv)
    drain(kv.at[pl.ds(0, 8)], next_recv)

    def attend(r):
        queries = (qq[r] * 0.125)[:, 0:64]
        scores, values = [], []
        for j in range(6):
            src = edge_ref[r, j]
            block = kv[jnp.clip(src - (dom - 1) * 8, 0, 23)]
            real = jnp.where(j < count_ref[r], fill_ref[src], 0)
            scores.append(jnp.where(lanes < real, mul(queries, block[0:64]), -1e30))
            values.append(jnp.concatenate([ones16, block[64:128]], axis=0))
        top = functools.reduce(jnp.maximum, scores)
        top = jnp.max(top, axis=1, keepdims=True)
        weights = [jnp.exp(s - top).astype(BF16) for s in scores]
        total = mul(jnp.concatenate(values, axis=1), jnp.concatenate(weights, axis=1), NT)
        local[r] = total[16:80] / total[0:1]

    for r in range(4):
        attend(r)

    @pl.when(middle)
    def _():
        either(x == 0, xs, 1, 3, xs_recv)
        ag[own] = sum(xs[i].astype(F32) for i in range(4)).astype(BF16)
        for device in near:
            fan(ag, own, own, ag_send, ag_recv, device)

    for r in range(4, 8):
        attend(r)

    one, two = jnp.logical_and(middle, x > 0), jnp.logical_and(middle, x == 0)
    for case, count in ((jnp.logical_not(middle), 10), (one, 9), (two, 8)):

        @pl.when(case)
        def _():
            drain(tally.at[pl.ds(0, count)], ag_recv)

    stack = [jnp.concatenate([ag[0, 16:32], ag[1, 16:32]], axis=1)]
    stack += [jnp.concatenate([ag[2 * g, 0:16], ag[2 * g + 1, 0:16]], axis=1) for g in range(4)]
    whole = jnp.concatenate(stack, axis=0)

    def mix(r):
        both = mul(whole, phiq[r])
        return (local[r] + both[16:80] / both[0:1]).astype(BF16)

    for o in (4, 5, 2, 3, 6, 7, 1):
        to = head ^ o
        mixed[o - 1] = mix(to)
        push(mixed.at[o - 1], ret.at[head], a_send, a_recv, (dom, to))
    ret[head] = mix(head)
    drain(mixed, a_recv)

    drain(xg.at[pl.ds(0, 3)], x_send)
    drain(wt.at[0], w_send)
    drain(kv.at[pl.ds(0, 16)], n_send)
    drain(kv.at[pl.ds(0, 8)], m_send)

    @pl.when(middle)
    def _():
        either(x == 0, xs, 1, 3, xs_send)
        either(x == 0, rs, 0, CUBE - 1, ag_send)

    for case, count in ((jnp.logical_not(middle), 10), (one, 9), (two, 8)):

        @pl.when(case)
        def _():
            drain(tally.at[pl.ds(0, count)], rs_send)

    drain(mixed, a_send)


def shards(
    node_feats, norm_gain, w_qkv, w_out, rand_feat, temper, edge_src, edge_count, block_fill
):
    dma = pltpu.SemaphoreType.DMA
    back = pl.pallas_call(
        kernel,
        out_shape=pltpu.VMEM((HEADS, 64, 128), BF16),
        in_specs=[pl.BlockSpec(memory_space=pltpu.HBM)] * 8,
        out_specs=pl.BlockSpec(memory_space=pltpu.VMEM),
        scratch_shapes=[
            pltpu.VMEM((1, 512), F32),
            pltpu.VMEM((1, 1), F32),
            pltpu.SMEM((8, 6), jnp.int32),
            pltpu.SMEM((8,), jnp.int32),
            pltpu.SMEM((512,), jnp.int32),
            pltpu.VMEM((128, 512), BF16),
                pltpu.VMEM((64, 256), F32),
            pltpu.VMEM((256, 128), BF16),
            pltpu.VMEM((NY, 128, 512), BF16),
            pltpu.VMEM((2, 192, 512), BF16),
            pltpu.VMEM((24, 128, 128), BF16),
            pltpu.VMEM((8, 128, 128), BF16),
            pltpu.VMEM((NY, 128, 128), BF16),
            pltpu.VMEM((NY, 128, 128), BF16),
            pltpu.VMEM((8, 256, 128), BF16),
            pltpu.VMEM((PARTS, 32, 128), BF16),
            pltpu.VMEM((CUBE, 32, 128), BF16),
            pltpu.VMEM((4, 32, 128), BF16),
            pltpu.VMEM((PARTS, 32, 128), BF16),
            pltpu.VMEM((10, 16, 128), BF16),
            pltpu.VMEM((8, 64, 128), F32),
            pltpu.VMEM((HEADS - 1, 64, 128), BF16),
            dma((8,)),
            dma, dma((NY - 1,)),
            dma, dma,
            dma, dma, dma,
            dma, dma((NY,)), dma,
            dma, dma, dma, dma, dma, dma, dma, dma,
        ],
        compiler_params=pltpu.CompilerParams(
            collective_id=0, has_side_effects=True, vmem_limit_bytes=56 * 2**20
        ),
        name="graph_layer",
    )(
        node_feats, norm_gain.reshape(1, -1), w_qkv.T, rand_feat[0], temper.reshape(1, 1), edge_src,
        edge_count, block_fill,
    )
    return lax.dot_general(
        back.reshape(512, 128), w_out, (((0,), (0,)), ((), ())), preferred_element_type=F32
    ).astype(BF16)


def solution(mesh):
    return jax.shard_map(
        shards,
        mesh=mesh,
        in_specs=(
            P(("dom", "head"), None),
            P(),
            P(None, "head"),
            P(),
            P("head", None, None),
            P("head"),
            P("dom", None),
            P("dom"),
            P(),
        ),
        out_specs=P(("dom", "head"), None),
        check_vma=False,
    )
```

```python
import functools
import math

import jax
import jax.numpy as jnp
from jax import lax
from jax.experimental import pallas as pl
from jax.experimental.pallas import tpu as pltpu
from jax.sharding import PartitionSpec as P

BLK = 128
NX, NZ, NY = 4, 16, 4
QUAD = 4
CUBE = NX * QUAD
PARTS = 8
HEADS = 2 * NY
BF16 = jnp.bfloat16
F32 = jnp.float32
MESH = pl.DeviceIdType.MESH
NT = (((1,), (1,)), ((), ()))
NN = (((1,), (0,)), ((), ()))


def mul(a, b, dims=NN):
    return lax.dot_general(a, b, dims, preferred_element_type=F32)


def kernel(
    feats_hbm, gain_hbm, w_hbm, rand_hbm, temper_hbm, edge_hbm, count_hbm, fill_hbm,
    ret,
    gain, temper_ref, edge_ref, count_ref, fill_ref, feats, rand, rot, xg, wt, kv, qq, mkv, mq, phiq, parts, rs, xs, ag, tally, local, mixed,
    load_sem, x_send, x_recv, w_send, w_recv, n_send, prev_recv, next_recv,
    m_send, mk_recv, mq_recv, rs_send, rs_recv, xs_send, xs_recv, ag_send, ag_recv,
    a_send, a_recv,
):
    dom = lax.axis_index("dom")
    head = lax.axis_index("head")
    y, c = head // 2, head % 2
    x, z = dom // NZ, dom % NZ
    mate = y * 2 + (1 - c)
    n_dom = NX * NZ
    right, left = (dom + 1) % n_dom, (dom + n_dom - 1) % n_dom

    loads = [
        pltpu.make_async_copy(feats_hbm, feats, load_sem.at[0]),
        pltpu.make_async_copy(w_hbm, wt.at[0], load_sem.at[1]),
        pltpu.make_async_copy(rand_hbm, rand, load_sem.at[2]),
        pltpu.make_async_copy(gain_hbm, gain, load_sem.at[3]),
        pltpu.make_async_copy(temper_hbm, temper_ref, load_sem.at[4]),
        pltpu.make_async_copy(edge_hbm, edge_ref, load_sem.at[5]),
        pltpu.make_async_copy(count_hbm, count_ref, load_sem.at[6]),
        pltpu.make_async_copy(fill_hbm, fill_ref, load_sem.at[7]),
    ]
    barrier = pltpu.get_barrier_semaphore()
    friends = [(d, h) for d in (left, right) for h in (head, mate)]
    quad, low = z // QUAD, z % QUAD
    place = x * QUAD + low
    middle = (low + 1) // 2 == 1
    own = x * 2 + (low + 1) % 2
    near = [
        (((x + i) % NX) * NZ + quad * QUAD + (low + j) % QUAD, head)
        for i in (2, 1, 3, 0)
        for j in (3, 1, 2, 0)
        if i or j
    ]
    far = [(x * NZ + (z + QUAD * o) % NZ, head) for o in (2, 1, 3)]
    friends = far + [(dom, head ^ o) for o in (4, 5, 2, 3, 6, 7, 1)] + friends + near
    for friend in friends:
        pl.semaphore_signal(barrier, inc=1, device_id=friend, device_id_type=MESH)

    for load in loads:
        load.start()

    def push(src, dst, send, recv, device):
        copy = pltpu.make_async_remote_copy(
            src_ref=src, dst_ref=dst, send_sem=send, recv_sem=recv,
            device_id=device, device_id_type=MESH,
        )
        copy.start()

    def drain(like, sem):
        pltpu.make_async_copy(like, like, sem).wait()

    def thin(ref, i):
        return ref.at[i, pl.ds(0, 16)]

    def either(wide, ref, start, count, sem):
        @pl.when(wide)
        def _():
            drain(ref.at[pl.ds(start, count)], sem)

        @pl.when(jnp.logical_not(wide))
        def _():
            drain(ref.at[pl.ds(start, count), pl.ds(0, 16)], sem)

    def fan(ref, here, there, send, recv, device):
        @pl.when(x == 0)
        def _():
            push(ref.at[here], ref.at[there], send, recv, device)

        @pl.when(x > 0)
        def _():
            push(thin(ref, here), thin(ref, there), send, recv, device)

    loads[0].wait()
    loads[3].wait()
    rows = feats[...].astype(F32)
    centred = rows - jnp.mean(rows, axis=-1, keepdims=True)
    spread = jnp.mean(centred * centred, axis=-1, keepdims=True)
    xg[0] = (centred * lax.rsqrt(spread + 1e-05) * gain[...]).astype(BF16)

    loads[1].wait()

    pl.semaphore_wait(barrier, len(friends))
    for o in range(1, NY):
        push(xg.at[0], xg.at[o], x_send, x_recv.at[o - 1], (dom, ((y + o) % NY) * 2 + c))
    push(wt.at[0], wt.at[1], w_send, w_recv, (dom, mate))

    loads[2].wait()
    for i in range(4, 8):
        loads[i].wait()
    temper = temper_ref[...]
    scaled = rand[...] * (jnp.sqrt(temper) * 64 ** (-0.25))
    coarse = scaled.astype(BF16).astype(F32)
    rot[...] = jnp.concatenate([coarse, scaled - coarse], axis=0).T.astype(BF16)
    half = temper * (1.0 / 16.0)
    log_root = math.log(16.0)

    lanes = lax.broadcasted_iota(jnp.int32, (8, 128), 1)[0:1]
    ones16 = jnp.ones((16, 128), BF16)
    rotated = rot[...]

    def key_features(r):
        both = kv[8 + r]
        keys = both[0:64]
        wide = keys.astype(F32)
        norm = jnp.sum(wide * wide, axis=0, keepdims=True)
        lifted = mul(rotated, jnp.concatenate([keys, keys], axis=0))
        phi = jnp.exp(lifted - (norm * half + log_root))
        phi = jnp.where(lanes < fill_ref[dom * 8 + r], phi, 0.0).astype(BF16)
        return phi, jnp.concatenate([ones16, both[64:128]], axis=0)

    def pair_sums(o):
        first = ((y + NY - o) % NY) * 2
        one = key_features(first + c)
        drain(mkv.at[o], mk_recv.at[o])
        two = key_features(first + 1 - c)
        return mul(
            jnp.concatenate([one[1], two[1]], axis=1),
            jnp.concatenate([one[0], two[0]], axis=1),
            NT,
        )


    def share(o):
        r = ((y + NY - o) % NY) * 2 + c
        for d, base, sem in ((right, 0, prev_recv), (left, 16, next_recv)):
            push(kv.at[8 + r], kv.at[base + r], n_send, sem, (d, head))
            push(mkv.at[o], kv.at[base + r], n_send, sem, (d, mate))

    drain(wt.at[1], w_recv)
    order = (0, 1, 3, 2)
    sums = jnp.zeros((80, 256), F32)
    for n, o in enumerate(order):
        if n == 3:
            sums += pair_sums(order[2])
        if o > 0:
            drain(xg.at[o], x_recv.at[o - 1])
        r = ((y + NY - o) % NY) * 2 + c
        wkv = jnp.concatenate([wt[0, 64:192], wt[1, 64:192]], axis=0)
        kv2 = mul(wkv, xg[o], NT).astype(BF16)
        mkv[o] = kv2[128:256]
        push(mkv.at[o], kv.at[8 + r], m_send, mk_recv.at[o], (dom, mate))
        kv[8 + r] = kv2[0:128]
        if n < 3:
            share(o)
        if n in (1, 2):
            sums += pair_sums(order[n - 1])
    sums += pair_sums(order[-1])
    rounded = sums.astype(BF16)
    for k in range(PARTS):
        g, columns = k // 2, slice(128 * (k % 2), 128 * (k % 2) + 128)
        parts[k, 0:16] = rounded[16 + 16 * g : 32 + 16 * g, columns]
        parts[k, 16:32] = rounded[0:16, columns]

    @pl.when(middle)
    def _():
        rs[place] = parts[own]

    for i in (2, 1, 3, 0):
        for j in (1, 2):
            to = (x + i) % NX

            @pl.when((low != j) if i == 0 else (low >= 0))
            def _():
                device = (to * NZ + quad * QUAD + j, head)
                part = to * 2 + j - 1

                @pl.when(to == 0)
                def _():
                    push(parts.at[part], rs.at[place], rs_send, rs_recv, device)

                @pl.when(to > 0)
                def _():
                    push(thin(parts, part), thin(rs, place), rs_send, rs_recv, device)

    share(order[-1])

    wq = jnp.concatenate([wt[i, 0:64] for i in (0, 0, 1, 1)], axis=0)
    for o in order:
        r = ((y + NY - o) % NY) * 2 + c
        q2 = mul(xg[o], wq, NT).astype(BF16)
        mq[o] = q2[:, 128:256]
        push(mq.at[o], qq.at[r], m_send, mq_recv, (dom, mate))
        qq[r] = q2[:, 0:128]
    side = lax.broadcasted_iota(jnp.int32, (128, 128), 1) < 64

    def query_features(r):
        rows_q = qq[r]
        wide = rows_q.astype(F32)
        square = wide * wide
        top = square.astype(BF16)
        rest = (square - top.astype(F32)).astype(BF16)
        norm = mul(ones16, jnp.where(side, top, rest), NT)[0:1]
        lifted = mul(rotated, rows_q, NT)
        phiq[r] = jnp.exp(lifted - (norm * half + log_root)).astype(BF16)

    for i in range(NY):
        query_features(2 * i + c)
    drain(mkv, mq_recv)
    for i in range(NY):
        query_features(2 * i + (1 - c))

    @pl.when(middle)
    def _():
        either(x == 0, rs, 0, CUBE - 1, rs_recv)
        xs[0] = sum(rs[i].astype(F32) for i in range(CUBE)).astype(BF16)
        for slot, device in enumerate(far):
            fan(xs, 0, 1 + slot, xs_send, xs_recv, device)

    drain(kv.at[pl.ds(0, 8)], prev_recv)
    drain(kv.at[pl.ds(0, 8)], next_recv)

    def attend(r):
        queries = (qq[r] * 0.125)[:, 0:64]
        scores, values = [], []
        for j in range(6):
            src = edge_ref[r, j]
            block = kv[jnp.clip(src - (dom - 1) * 8, 0, 23)]
            real = jnp.where(j < count_ref[r], fill_ref[src], 0)
            scores.append(jnp.where(lanes < real, mul(queries, block[0:64]), -1e30))
            values.append(jnp.concatenate([ones16, block[64:128]], axis=0))
        top = functools.reduce(jnp.maximum, scores)
        top = jnp.max(top, axis=1, keepdims=True)
        weights = [jnp.exp(s - top).astype(BF16) for s in scores]
        total = mul(jnp.concatenate(values, axis=1), jnp.concatenate(weights, axis=1), NT)
        local[r] = total[16:80] / total[0:1]

    for r in range(4):
        attend(r)

    @pl.when(middle)
    def _():
        either(x == 0, xs, 1, 3, xs_recv)
        ag[own] = sum(xs[i].astype(F32) for i in range(4)).astype(BF16)
        for j in range(QUAD):
            for i in (2, 1, 3, 0):

                @pl.when((low != j) if i == 0 else (low >= 0))
                def _():
                    device = (((x + i) % NX) * NZ + quad * QUAD + j, head)
                    fan(ag, own, own, ag_send, ag_recv, device)

    for r in range(4, 8):
        attend(r)

    one, two = jnp.logical_and(middle, x > 0), jnp.logical_and(middle, x == 0)
    for case, count in ((jnp.logical_not(middle), 10), (one, 9), (two, 8)):

        @pl.when(case)
        def _():
            drain(tally.at[pl.ds(0, count)], ag_recv)

    stack = [jnp.concatenate([ag[0, 16:32], ag[1, 16:32]], axis=1)]
    stack += [jnp.concatenate([ag[2 * g, 0:16], ag[2 * g + 1, 0:16]], axis=1) for g in range(4)]
    whole = jnp.concatenate(stack, axis=0)

    def mix(r):
        both = mul(whole, phiq[r])
        return (local[r] + both[16:80] / both[0:1]).astype(BF16)

    for to in (1, 0, 3, 2, 5, 4, 7, 6):

        @pl.when(head == to)
        def _():
            ret[to] = mix(to)

        @pl.when(head != to)
        def _():
            mixed[to] = mix(to)
            push(mixed.at[to], ret.at[head], a_send, a_recv, (dom, to))

    drain(mixed.at[pl.ds(0, HEADS - 1)], a_recv)

    drain(xg.at[pl.ds(0, 3)], x_send)
    drain(wt.at[0], w_send)
    drain(kv.at[pl.ds(0, 16)], n_send)
    drain(kv.at[pl.ds(0, 8)], m_send)

    @pl.when(middle)
    def _():
        either(x == 0, xs, 1, 3, xs_send)
        either(x == 0, rs, 0, CUBE - 1, ag_send)

    for case, count in ((jnp.logical_not(middle), 10), (one, 9), (two, 8)):

        @pl.when(case)
        def _():
            drain(tally.at[pl.ds(0, count)], rs_send)

    drain(mixed.at[pl.ds(0, HEADS - 1)], a_send)


def shards(
    node_feats, norm_gain, w_qkv, w_out, rand_feat, temper, edge_src, edge_count, block_fill
):
    dma = pltpu.SemaphoreType.DMA
    back = pl.pallas_call(
        kernel,
        out_shape=pltpu.VMEM((HEADS, 64, 128), BF16),
        in_specs=[pl.BlockSpec(memory_space=pltpu.HBM)] * 8,
        out_specs=pl.BlockSpec(memory_space=pltpu.VMEM),
        scratch_shapes=[
            pltpu.VMEM((1, 512), F32),
            pltpu.VMEM((1, 1), F32),
            pltpu.SMEM((8, 6), jnp.int32),
            pltpu.SMEM((8,), jnp.int32),
            pltpu.SMEM((512,), jnp.int32),
            pltpu.VMEM((128, 512), BF16),
                pltpu.VMEM((64, 256), F32),
            pltpu.VMEM((256, 128), BF16),
            pltpu.VMEM((NY, 128, 512), BF16),
            pltpu.VMEM((2, 192, 512), BF16),
            pltpu.VMEM((24, 128, 128), BF16),
            pltpu.VMEM((8, 128, 128), BF16),
            pltpu.VMEM((NY, 128, 128), BF16),
            pltpu.VMEM((NY, 128, 128), BF16),
            pltpu.VMEM((8, 256, 128), BF16),
            pltpu.VMEM((PARTS, 32, 128), BF16),
            pltpu.VMEM((CUBE, 32, 128), BF16),
            pltpu.VMEM((4, 32, 128), BF16),
            pltpu.VMEM((PARTS, 32, 128), BF16),
            pltpu.VMEM((10, 16, 128), BF16),
            pltpu.VMEM((8, 64, 128), F32),
            pltpu.VMEM((HEADS, 64, 128), BF16),
            dma((8,)),
            dma, dma((NY - 1,)),
            dma, dma,
            dma, dma, dma,
            dma, dma((NY,)), dma,
            dma, dma, dma, dma, dma, dma, dma, dma,
        ],
        compiler_params=pltpu.CompilerParams(
            collective_id=0, has_side_effects=True, vmem_limit_bytes=56 * 2**20
        ),
        name="graph_layer",
    )(
        node_feats, norm_gain.reshape(1, -1), w_qkv.T, rand_feat[0], temper.reshape(1, 1), edge_src,
        edge_count, block_fill,
    )
    return lax.dot_general(
        back.reshape(512, 128), w_out, (((0,), (0,)), ((), ())), preferred_element_type=F32
    ).astype(BF16)


def solution(mesh):
    return jax.shard_map(
        shards,
        mesh=mesh,
        in_specs=(
            P(("dom", "head"), None),
            P(),
            P(None, "head"),
            P(),
            P("head", None, None),
            P("head"),
            P("dom", None),
            P("dom"),
            P(),
        ),
        out_specs=P(("dom", "head"), None),
        check_vma=False,
    )
```

```python
import functools
import math

import jax
import jax.numpy as jnp
from jax import lax
from jax.experimental import pallas as pl
from jax.experimental.pallas import tpu as pltpu
from jax.sharding import PartitionSpec as P

BLK = 128
NX, NZ, NY = 4, 16, 4
QUAD = 4
CUBE = NX * QUAD
PARTS = 8
HEADS = 2 * NY
BF16 = jnp.bfloat16
F32 = jnp.float32
MESH = pl.DeviceIdType.MESH
NT = (((1,), (1,)), ((), ()))
NN = (((1,), (0,)), ((), ()))


def mul(a, b, dims=NN):
    return lax.dot_general(a, b, dims, preferred_element_type=F32)


def kernel(
    feats_hbm, gain_hbm, w_hbm, rand_hbm, temper_hbm, edge_hbm, count_hbm, fill_hbm,
    ret,
    gain, temper_ref, edge_ref, count_ref, fill_ref, feats, rand, rot, xg, wt, kv, qq, mkv, mq, phiq, parts, rs, xs, ag, tally, local, mixed,
    load_sem, x_send, x_recv, w_send, w_recv, n_send, prev_recv, next_recv,
    m_send, mk_recv, mq_recv, rs_send, rs_recv, xs_send, xs_recv, ag_send, ag_recv,
    a_send, a_recv,
):
    dom = lax.axis_index("dom")
    head = lax.axis_index("head")
    y, c = head // 2, head % 2
    x, z = dom // NZ, dom % NZ
    mate = y * 2 + (1 - c)
    n_dom = NX * NZ
    right, left = (dom + 1) % n_dom, (dom + n_dom - 1) % n_dom

    loads = [
        pltpu.make_async_copy(feats_hbm, feats, load_sem.at[0]),
        pltpu.make_async_copy(w_hbm, wt.at[0], load_sem.at[1]),
        pltpu.make_async_copy(rand_hbm, rand, load_sem.at[2]),
        pltpu.make_async_copy(gain_hbm, gain, load_sem.at[3]),
        pltpu.make_async_copy(temper_hbm, temper_ref, load_sem.at[4]),
        pltpu.make_async_copy(edge_hbm, edge_ref, load_sem.at[5]),
        pltpu.make_async_copy(count_hbm, count_ref, load_sem.at[6]),
        pltpu.make_async_copy(fill_hbm, fill_ref, load_sem.at[7]),
    ]
    barrier = pltpu.get_barrier_semaphore()
    friends = [(d, h) for d in (left, right) for h in (head, mate)]
    quad, low = z // QUAD, z % QUAD
    place = x * QUAD + low
    middle = low < 2
    own = x * 2 + low % 2
    near = [
        (((x + i) % NX) * NZ + quad * QUAD + (low + j) % QUAD, head)
        for i in (2, 1, 3, 0)
        for j in (3, 1, 2, 0)
        if i or j
    ]
    far = [(x * NZ + (z + QUAD * o) % NZ, head) for o in (2, 1, 3)]
    friends = far + [(dom, head ^ o) for o in (4, 5, 2, 3, 6, 7, 1)] + friends + near
    for friend in friends:
        pl.semaphore_signal(barrier, inc=1, device_id=friend, device_id_type=MESH)

    for load in loads:
        load.start()

    def push(src, dst, send, recv, device):
        copy = pltpu.make_async_remote_copy(
            src_ref=src, dst_ref=dst, send_sem=send, recv_sem=recv,
            device_id=device, device_id_type=MESH,
        )
        copy.start()

    def drain(like, sem):
        pltpu.make_async_copy(like, like, sem).wait()

    def thin(ref, i):
        return ref.at[i, pl.ds(0, 16)]

    def either(wide, ref, start, count, sem):
        @pl.when(wide)
        def _():
            drain(ref.at[pl.ds(start, count)], sem)

        @pl.when(jnp.logical_not(wide))
        def _():
            drain(ref.at[pl.ds(start, count), pl.ds(0, 16)], sem)

    def fan(ref, here, there, send, recv, device):
        @pl.when(x == 0)
        def _():
            push(ref.at[here], ref.at[there], send, recv, device)

        @pl.when(x > 0)
        def _():
            push(thin(ref, here), thin(ref, there), send, recv, device)

    loads[0].wait()
    loads[3].wait()
    rows = feats[...].astype(F32)
    centred = rows - jnp.mean(rows, axis=-1, keepdims=True)
    spread = jnp.mean(centred * centred, axis=-1, keepdims=True)
    xg[0] = (centred * lax.rsqrt(spread + 1e-05) * gain[...]).astype(BF16)

    loads[1].wait()

    pl.semaphore_wait(barrier, len(friends))
    for o in range(1, NY):
        push(xg.at[0], xg.at[o], x_send, x_recv.at[o - 1], (dom, ((y + o) % NY) * 2 + c))
    push(wt.at[0], wt.at[1], w_send, w_recv, (dom, mate))

    loads[2].wait()
    for i in range(4, 8):
        loads[i].wait()
    temper = temper_ref[...]
    scaled = rand[...] * (jnp.sqrt(temper) * 64 ** (-0.25))
    coarse = scaled.astype(BF16).astype(F32)
    rot[...] = jnp.concatenate([coarse, scaled - coarse], axis=0).T.astype(BF16)
    half = temper * (1.0 / 16.0)
    log_root = math.log(16.0)

    lanes = lax.broadcasted_iota(jnp.int32, (8, 128), 1)[0:1]
    ones16 = jnp.ones((16, 128), BF16)
    rotated = rot[...]

    def key_features(r):
        both = kv[8 + r]
        keys = both[0:64]
        wide = keys.astype(F32)
        norm = jnp.sum(wide * wide, axis=0, keepdims=True)
        lifted = mul(rotated, jnp.concatenate([keys, keys], axis=0))
        phi = jnp.exp(lifted - (norm * half + log_root))
        phi = jnp.where(lanes < fill_ref[dom * 8 + r], phi, 0.0).astype(BF16)
        return phi, jnp.concatenate([ones16, both[64:128]], axis=0)

    def pair_sums(o):
        first = ((y + NY - o) % NY) * 2
        one = key_features(first + c)
        drain(mkv.at[o], mk_recv.at[o])
        two = key_features(first + 1 - c)
        return mul(
            jnp.concatenate([one[1], two[1]], axis=1),
            jnp.concatenate([one[0], two[0]], axis=1),
            NT,
        )


    def share(o):
        r = ((y + NY - o) % NY) * 2 + c
        for d, base, sem in ((right, 0, prev_recv), (left, 16, next_recv)):
            push(kv.at[8 + r], kv.at[base + r], n_send, sem, (d, head))
            push(mkv.at[o], kv.at[base + r], n_send, sem, (d, mate))

    drain(wt.at[1], w_recv)
    order = (0, 1, 3, 2)
    sums = jnp.zeros((80, 256), F32)
    for n, o in enumerate(order):
        if n == 3:
            sums += pair_sums(order[2])
        if o > 0:
            drain(xg.at[o], x_recv.at[o - 1])
        r = ((y + NY - o) % NY) * 2 + c
        wkv = jnp.concatenate([wt[0, 64:192], wt[1, 64:192]], axis=0)
        kv2 = mul(wkv, xg[o], NT).astype(BF16)
        mkv[o] = kv2[128:256]
        push(mkv.at[o], kv.at[8 + r], m_send, mk_recv.at[o], (dom, mate))
        kv[8 + r] = kv2[0:128]
        if n < 3:
            share(o)
        if n in (1, 2):
            sums += pair_sums(order[n - 1])
    sums += pair_sums(order[-1])
    rounded = sums.astype(BF16)
    for k in range(PARTS):
        g, columns = k // 2, slice(128 * (k % 2), 128 * (k % 2) + 128)
        parts[k, 0:16] = rounded[16 + 16 * g : 32 + 16 * g, columns]
        parts[k, 16:32] = rounded[0:16, columns]

    @pl.when(middle)
    def _():
        rs[place] = parts[own]

    for i in (2, 1, 3, 0):
        for j in (0, 1):
            to = (x + i) % NX

            @pl.when((low != j) if i == 0 else (low >= 0))
            def _():
                device = (to * NZ + quad * QUAD + j, head)
                part = to * 2 + j

                @pl.when(to == 0)
                def _():
                    push(parts.at[part], rs.at[place], rs_send, rs_recv, device)

                @pl.when(to > 0)
                def _():
                    push(thin(parts, part), thin(rs, place), rs_send, rs_recv, device)

    share(order[-1])

    wq = jnp.concatenate([wt[i, 0:64] for i in (0, 0, 1, 1)], axis=0)
    for o in order:
        r = ((y + NY - o) % NY) * 2 + c
        q2 = mul(xg[o], wq, NT).astype(BF16)
        mq[o] = q2[:, 128:256]
        push(mq.at[o], qq.at[r], m_send, mq_recv, (dom, mate))
        qq[r] = q2[:, 0:128]
    side = lax.broadcasted_iota(jnp.int32, (128, 128), 1) < 64

    def query_features(r):
        rows_q = qq[r]
        wide = rows_q.astype(F32)
        square = wide * wide
        top = square.astype(BF16)
        rest = (square - top.astype(F32)).astype(BF16)
        norm = mul(ones16, jnp.where(side, top, rest), NT)[0:1]
        lifted = mul(rotated, rows_q, NT)
        phiq[r] = jnp.exp(lifted - (norm * half + log_root)).astype(BF16)

    for i in range(NY):
        query_features(2 * i + c)
    drain(mkv, mq_recv)
    for i in range(NY):
        query_features(2 * i + (1 - c))

    @pl.when(middle)
    def _():
        either(x == 0, rs, 0, CUBE - 1, rs_recv)
        xs[0] = sum(rs[i].astype(F32) for i in range(CUBE)).astype(BF16)
        for slot, device in enumerate(far):
            fan(xs, 0, 1 + slot, xs_send, xs_recv, device)

    drain(kv.at[pl.ds(0, 8)], prev_recv)
    drain(kv.at[pl.ds(0, 8)], next_recv)

    def attend(r):
        queries = (qq[r] * 0.125)[:, 0:64]
        scores, values = [], []
        for j in range(6):
            src = edge_ref[r, j]
            block = kv[jnp.clip(src - (dom - 1) * 8, 0, 23)]
            real = jnp.where(j < count_ref[r], fill_ref[src], 0)
            scores.append(jnp.where(lanes < real, mul(queries, block[0:64]), -1e30))
            values.append(jnp.concatenate([ones16, block[64:128]], axis=0))
        top = functools.reduce(jnp.maximum, scores)
        top = jnp.max(top, axis=1, keepdims=True)
        weights = [jnp.exp(s - top).astype(BF16) for s in scores]
        total = mul(jnp.concatenate(values, axis=1), jnp.concatenate(weights, axis=1), NT)
        local[r] = total[16:80] / total[0:1]

    for r in range(4):
        attend(r)

    @pl.when(middle)
    def _():
        either(x == 0, xs, 1, 3, xs_recv)
        ag[own] = sum(xs[i].astype(F32) for i in range(4)).astype(BF16)
        for j in range(QUAD):
            for i in (2, 1, 3, 0):

                @pl.when((low != j) if i == 0 else (low >= 0))
                def _():
                    device = (((x + i) % NX) * NZ + quad * QUAD + j, head)
                    fan(ag, own, own, ag_send, ag_recv, device)

    for r in range(4, 8):
        attend(r)

    one, two = jnp.logical_and(middle, x > 0), jnp.logical_and(middle, x == 0)
    for case, count in ((jnp.logical_not(middle), 10), (one, 9), (two, 8)):

        @pl.when(case)
        def _():
            drain(tally.at[pl.ds(0, count)], ag_recv)

    stack = [jnp.concatenate([ag[0, 16:32], ag[1, 16:32]], axis=1)]
    stack += [jnp.concatenate([ag[2 * g, 0:16], ag[2 * g + 1, 0:16]], axis=1) for g in range(4)]
    whole = jnp.concatenate(stack, axis=0)

    def mix(r):
        both = mul(whole, phiq[r])
        return (local[r] + both[16:80] / both[0:1]).astype(BF16)

    for to in (1, 0, 3, 2, 5, 4, 7, 6):

        @pl.when(head == to)
        def _():
            ret[to] = mix(to)

        @pl.when(head != to)
        def _():
            mixed[to] = mix(to)
            push(mixed.at[to], ret.at[head], a_send, a_recv, (dom, to))

    drain(mixed.at[pl.ds(0, HEADS - 1)], a_recv)

    drain(xg.at[pl.ds(0, 3)], x_send)
    drain(wt.at[0], w_send)
    drain(kv.at[pl.ds(0, 16)], n_send)
    drain(kv.at[pl.ds(0, 8)], m_send)

    @pl.when(middle)
    def _():
        either(x == 0, xs, 1, 3, xs_send)
        either(x == 0, rs, 0, CUBE - 1, ag_send)

    for case, count in ((jnp.logical_not(middle), 10), (one, 9), (two, 8)):

        @pl.when(case)
        def _():
            drain(tally.at[pl.ds(0, count)], rs_send)

    drain(mixed.at[pl.ds(0, HEADS - 1)], a_send)


def shards(
    node_feats, norm_gain, w_qkv, w_out, rand_feat, temper, edge_src, edge_count, block_fill
):
    dma = pltpu.SemaphoreType.DMA
    back = pl.pallas_call(
        kernel,
        out_shape=pltpu.VMEM((HEADS, 64, 128), BF16),
        in_specs=[pl.BlockSpec(memory_space=pltpu.HBM)] * 8,
        out_specs=pl.BlockSpec(memory_space=pltpu.VMEM),
        scratch_shapes=[
            pltpu.VMEM((1, 512), F32),
            pltpu.VMEM((1, 1), F32),
            pltpu.SMEM((8, 6), jnp.int32),
            pltpu.SMEM((8,), jnp.int32),
            pltpu.SMEM((512,), jnp.int32),
            pltpu.VMEM((128, 512), BF16),
                pltpu.VMEM((64, 256), F32),
            pltpu.VMEM((256, 128), BF16),
            pltpu.VMEM((NY, 128, 512), BF16),
            pltpu.VMEM((2, 192, 512), BF16),
            pltpu.VMEM((24, 128, 128), BF16),
            pltpu.VMEM((8, 128, 128), BF16),
            pltpu.VMEM((NY, 128, 128), BF16),
            pltpu.VMEM((NY, 128, 128), BF16),
            pltpu.VMEM((8, 256, 128), BF16),
            pltpu.VMEM((PARTS, 32, 128), BF16),
            pltpu.VMEM((CUBE, 32, 128), BF16),
            pltpu.VMEM((4, 32, 128), BF16),
            pltpu.VMEM((PARTS, 32, 128), BF16),
            pltpu.VMEM((10, 16, 128), BF16),
            pltpu.VMEM((8, 64, 128), F32),
            pltpu.VMEM((HEADS, 64, 128), BF16),
            dma((8,)),
            dma, dma((NY - 1,)),
            dma, dma,
            dma, dma, dma,
            dma, dma((NY,)), dma,
            dma, dma, dma, dma, dma, dma, dma, dma,
        ],
        compiler_params=pltpu.CompilerParams(
            collective_id=0, has_side_effects=True, vmem_limit_bytes=56 * 2**20
        ),
        name="graph_layer",
    )(
        node_feats, norm_gain.reshape(1, -1), w_qkv.T, rand_feat[0], temper.reshape(1, 1), edge_src,
        edge_count, block_fill,
    )
    return lax.dot_general(
        back.reshape(512, 128), w_out, (((0,), (0,)), ((), ())), preferred_element_type=F32
    ).astype(BF16)


def solution(mesh):
    return jax.shard_map(
        shards,
        mesh=mesh,
        in_specs=(
            P(("dom", "head"), None),
            P(),
            P(None, "head"),
            P(),
            P("head", None, None),
            P("head"),
            P("dom", None),
            P("dom"),
            P(),
        ),
        out_specs=P(("dom", "head"), None),
        check_vma=False,
    )
```

```python
import functools
import math

import jax
import jax.numpy as jnp
from jax import lax
from jax.experimental import pallas as pl
from jax.experimental.pallas import tpu as pltpu
from jax.sharding import PartitionSpec as P

BLK = 128
NX, NZ, NY = 4, 16, 4
QUAD = 4
CUBE = NX * QUAD
PARTS = 8
HEADS = 2 * NY
BF16 = jnp.bfloat16
F32 = jnp.float32
MESH = pl.DeviceIdType.MESH
NT = (((1,), (1,)), ((), ()))
NN = (((1,), (0,)), ((), ()))


def mul(a, b, dims=NN):
    return lax.dot_general(a, b, dims, preferred_element_type=F32)


def kernel(
    feats_hbm, gain_hbm, w_hbm, rand_hbm, temper_hbm, edge_hbm, count_hbm, fill_hbm,
    ret,
    gain, temper_ref, edge_ref, count_ref, fill_ref, feats, rand, rot, xg, wt, kv, qq, mkv, mq, phiq, parts, rs, xs, ag, tally, local, mixed,
    load_sem, x_send, x_recv, w_send, w_recv, n_send, prev_recv, next_recv,
    m_send, mk_recv, mq_recv, rs_send, rs_recv, xs_send, xs_recv, ag_send, ag_recv,
    a_send, a_recv,
):
    dom = lax.axis_index("dom")
    head = lax.axis_index("head")
    y, c = head // 2, head % 2
    x, z = dom // NZ, dom % NZ
    mate = y * 2 + (1 - c)
    n_dom = NX * NZ
    right, left = (dom + 1) % n_dom, (dom + n_dom - 1) % n_dom

    loads = [
        pltpu.make_async_copy(feats_hbm, feats, load_sem.at[0]),
        pltpu.make_async_copy(w_hbm, wt.at[0], load_sem.at[1]),
        pltpu.make_async_copy(rand_hbm, rand, load_sem.at[2]),
        pltpu.make_async_copy(gain_hbm, gain, load_sem.at[3]),
        pltpu.make_async_copy(temper_hbm, temper_ref, load_sem.at[4]),
        pltpu.make_async_copy(edge_hbm, edge_ref, load_sem.at[5]),
        pltpu.make_async_copy(count_hbm, count_ref, load_sem.at[6]),
        pltpu.make_async_copy(fill_hbm, fill_ref, load_sem.at[7]),
    ]
    barrier = pltpu.get_barrier_semaphore()
    friends = [(d, h) for d in (left, right) for h in (head, mate)]
    quad, low = z // QUAD, z % QUAD
    place = x * QUAD + low
    middle = low < 2
    own = x * 2 + low % 2
    near = [
        (((x + i) % NX) * NZ + quad * QUAD + (low + j) % QUAD, head)
        for i in (2, 1, 3, 0)
        for j in (3, 1, 2, 0)
        if i or j
    ]
    far = [(x * NZ + (z + QUAD * o) % NZ, head) for o in (2, 1, 3)]
    friends = far + [(dom, head ^ o) for o in (4, 5, 2, 3, 6, 7, 1)] + friends + near
    for friend in friends:
        pl.semaphore_signal(barrier, inc=1, device_id=friend, device_id_type=MESH)

    for load in loads:
        load.start()

    def push(src, dst, send, recv, device):
        copy = pltpu.make_async_remote_copy(
            src_ref=src, dst_ref=dst, send_sem=send, recv_sem=recv,
            device_id=device, device_id_type=MESH,
        )
        copy.start()

    def drain(like, sem):
        pltpu.make_async_copy(like, like, sem).wait()

    def thin(ref, i):
        return ref.at[i, pl.ds(0, 16)]

    def either(wide, ref, start, count, sem):
        @pl.when(wide)
        def _():
            drain(ref.at[pl.ds(start, count)], sem)

        @pl.when(jnp.logical_not(wide))
        def _():
            drain(ref.at[pl.ds(start, count), pl.ds(0, 16)], sem)

    def fan(ref, here, there, send, recv, device):
        @pl.when(x == 0)
        def _():
            push(ref.at[here], ref.at[there], send, recv, device)

        @pl.when(x > 0)
        def _():
            push(thin(ref, here), thin(ref, there), send, recv, device)

    loads[0].wait()
    loads[3].wait()
    rows = feats[...].astype(F32)
    centred = rows - jnp.mean(rows, axis=-1, keepdims=True)
    spread = jnp.mean(centred * centred, axis=-1, keepdims=True)
    xg[0] = (centred * lax.rsqrt(spread + 1e-05) * gain[...]).astype(BF16)

    loads[1].wait()

    pl.semaphore_wait(barrier, len(friends))
    for o in range(1, NY):
        push(xg.at[0], xg.at[o], x_send, x_recv.at[o - 1], (dom, ((y + o) % NY) * 2 + c))
    push(wt.at[0], wt.at[1], w_send, w_recv, (dom, mate))

    loads[2].wait()
    for i in range(4, 8):
        loads[i].wait()
    temper = temper_ref[...]
    scaled = rand[...] * (jnp.sqrt(temper) * 64 ** (-0.25))
    coarse = scaled.astype(BF16).astype(F32)
    rot[...] = jnp.concatenate([coarse, scaled - coarse], axis=0).T.astype(BF16)
    half = temper * (1.0 / 16.0)
    log_root = math.log(16.0)

    lanes = lax.broadcasted_iota(jnp.int32, (8, 128), 1)[0:1]
    ones16 = jnp.ones((16, 128), BF16)
    rotated = rot[...]

    def key_features(r):
        both = kv[8 + r]
        keys = both[0:64]
        wide = keys.astype(F32)
        norm = jnp.sum(wide * wide, axis=0, keepdims=True)
        lifted = mul(rotated, jnp.concatenate([keys, keys], axis=0))
        phi = jnp.exp(lifted - (norm * half + log_root))
        phi = jnp.where(lanes < fill_ref[dom * 8 + r], phi, 0.0).astype(BF16)
        return phi, jnp.concatenate([ones16, both[64:128]], axis=0)

    def pair_sums(o):
        first = ((y + NY - o) % NY) * 2
        one = key_features(first + c)
        drain(mkv.at[o], mk_recv.at[o])
        two = key_features(first + 1 - c)
        return mul(
            jnp.concatenate([one[1], two[1]], axis=1),
            jnp.concatenate([one[0], two[0]], axis=1),
            NT,
        )


    def share(o):
        r = ((y + NY - o) % NY) * 2 + c
        for d, base, sem in ((right, 0, prev_recv), (left, 16, next_recv)):
            push(kv.at[8 + r], kv.at[base + r], n_send, sem, (d, head))
            push(mkv.at[o], kv.at[base + r], n_send, sem, (d, mate))

    drain(wt.at[1], w_recv)
    order = (0, 1, 3, 2)
    sums = jnp.zeros((80, 256), F32)
    for n, o in enumerate(order):
        if n == 3:
            sums += pair_sums(order[2])
        if o > 0:
            drain(xg.at[o], x_recv.at[o - 1])
        r = ((y + NY - o) % NY) * 2 + c
        wkv = jnp.concatenate([wt[0, 64:192], wt[1, 64:192]], axis=0)
        kv2 = mul(wkv, xg[o], NT).astype(BF16)
        mkv[o] = kv2[128:256]
        push(mkv.at[o], kv.at[8 + r], m_send, mk_recv.at[o], (dom, mate))
        kv[8 + r] = kv2[0:128]
        if n < 2:
            share(o)
        if n in (1, 2):
            sums += pair_sums(order[n - 1])
    sums += pair_sums(order[-1])
    rounded = sums.astype(BF16)
    for k in range(PARTS):
        g, columns = k // 2, slice(128 * (k % 2), 128 * (k % 2) + 128)
        parts[k, 0:16] = rounded[16 + 16 * g : 32 + 16 * g, columns]
        parts[k, 16:32] = rounded[0:16, columns]

    @pl.when(middle)
    def _():
        rs[place] = parts[own]

    for i in (2, 1, 3, 0):
        for j in (0, 1):
            to = (x + i) % NX

            @pl.when((low != j) if i == 0 else (low >= 0))
            def _():
                device = (to * NZ + quad * QUAD + j, head)
                part = to * 2 + j

                @pl.when(to == 0)
                def _():
                    push(parts.at[part], rs.at[place], rs_send, rs_recv, device)

                @pl.when(to > 0)
                def _():
                    push(thin(parts, part), thin(rs, place), rs_send, rs_recv, device)

    share(order[2])
    share(order[3])

    wq = jnp.concatenate([wt[i, 0:64] for i in (0, 0, 1, 1)], axis=0)
    for o in order:
        r = ((y + NY - o) % NY) * 2 + c
        q2 = mul(xg[o], wq, NT).astype(BF16)
        mq[o] = q2[:, 128:256]
        push(mq.at[o], qq.at[r], m_send, mq_recv, (dom, mate))
        qq[r] = q2[:, 0:128]
    side = lax.broadcasted_iota(jnp.int32, (128, 128), 1) < 64

    def query_features(r):
        rows_q = qq[r]
        wide = rows_q.astype(F32)
        square = wide * wide
        top = square.astype(BF16)
        rest = (square - top.astype(F32)).astype(BF16)
        norm = mul(ones16, jnp.where(side, top, rest), NT)[0:1]
        lifted = mul(rotated, rows_q, NT)
        phiq[r] = jnp.exp(lifted - (norm * half + log_root)).astype(BF16)

    for i in range(NY):
        query_features(2 * i + c)
    drain(mkv, mq_recv)
    for i in range(NY):
        query_features(2 * i + (1 - c))

    @pl.when(middle)
    def _():
        either(x == 0, rs, 0, CUBE - 1, rs_recv)
        xs[0] = sum(rs[i].astype(F32) for i in range(CUBE)).astype(BF16)
        for slot, device in enumerate(far):
            fan(xs, 0, 1 + slot, xs_send, xs_recv, device)

    drain(kv.at[pl.ds(0, 8)], prev_recv)
    drain(kv.at[pl.ds(0, 8)], next_recv)

    def attend(r):
        queries = (qq[r] * 0.125)[:, 0:64]
        scores, values = [], []
        for j in range(6):
            src = edge_ref[r, j]
            block = kv[jnp.clip(src - (dom - 1) * 8, 0, 23)]
            real = jnp.where(j < count_ref[r], fill_ref[src], 0)
            scores.append(jnp.where(lanes < real, mul(queries, block[0:64]), -1e30))
            values.append(jnp.concatenate([ones16, block[64:128]], axis=0))
        top = functools.reduce(jnp.maximum, scores)
        top = jnp.max(top, axis=1, keepdims=True)
        weights = [jnp.exp(s - top).astype(BF16) for s in scores]
        total = mul(jnp.concatenate(values, axis=1), jnp.concatenate(weights, axis=1), NT)
        local[r] = total[16:80] / total[0:1]

    for r in range(4):
        attend(r)

    @pl.when(middle)
    def _():
        either(x == 0, xs, 1, 3, xs_recv)
        ag[own] = sum(xs[i].astype(F32) for i in range(4)).astype(BF16)
        for j in range(QUAD):
            for i in range(NX):

                @pl.when(jnp.logical_or(low != j, x != i))
                def _():
                    device = (i * NZ + quad * QUAD + j, head)
                    fan(ag, own, own, ag_send, ag_recv, device)

    for r in range(4, 8):
        attend(r)

    one, two = jnp.logical_and(middle, x > 0), jnp.logical_and(middle, x == 0)
    for case, count in ((jnp.logical_not(middle), 10), (one, 9), (two, 8)):

        @pl.when(case)
        def _():
            drain(tally.at[pl.ds(0, count)], ag_recv)

    stack = [jnp.concatenate([ag[0, 16:32], ag[1, 16:32]], axis=1)]
    stack += [jnp.concatenate([ag[2 * g, 0:16], ag[2 * g + 1, 0:16]], axis=1) for g in range(4)]
    whole = jnp.concatenate(stack, axis=0)

    def mix(r):
        both = mul(whole, phiq[r])
        return (local[r] + both[16:80] / both[0:1]).astype(BF16)

    for to in (1, 0, 3, 2, 5, 4, 7, 6):

        @pl.when(head == to)
        def _():
            ret[to] = mix(to)

        @pl.when(head != to)
        def _():
            mixed[to] = mix(to)
            push(mixed.at[to], ret.at[head], a_send, a_recv, (dom, to))

    drain(mixed.at[pl.ds(0, HEADS - 1)], a_recv)

    drain(xg.at[pl.ds(0, 3)], x_send)
    drain(wt.at[0], w_send)
    drain(kv.at[pl.ds(0, 16)], n_send)
    drain(kv.at[pl.ds(0, 8)], m_send)

    @pl.when(middle)
    def _():
        either(x == 0, xs, 1, 3, xs_send)
        either(x == 0, rs, 0, CUBE - 1, ag_send)

    for case, count in ((jnp.logical_not(middle), 10), (one, 9), (two, 8)):

        @pl.when(case)
        def _():
            drain(tally.at[pl.ds(0, count)], rs_send)

    drain(mixed.at[pl.ds(0, HEADS - 1)], a_send)


def shards(
    node_feats, norm_gain, w_qkv, w_out, rand_feat, temper, edge_src, edge_count, block_fill
):
    dma = pltpu.SemaphoreType.DMA
    back = pl.pallas_call(
        kernel,
        out_shape=pltpu.VMEM((HEADS, 64, 128), BF16),
        in_specs=[pl.BlockSpec(memory_space=pltpu.HBM)] * 8,
        out_specs=pl.BlockSpec(memory_space=pltpu.VMEM),
        scratch_shapes=[
            pltpu.VMEM((1, 512), F32),
            pltpu.VMEM((1, 1), F32),
            pltpu.SMEM((8, 6), jnp.int32),
            pltpu.SMEM((8,), jnp.int32),
            pltpu.SMEM((512,), jnp.int32),
            pltpu.VMEM((128, 512), BF16),
                pltpu.VMEM((64, 256), F32),
            pltpu.VMEM((256, 128), BF16),
            pltpu.VMEM((NY, 128, 512), BF16),
            pltpu.VMEM((2, 192, 512), BF16),
            pltpu.VMEM((24, 128, 128), BF16),
            pltpu.VMEM((8, 128, 128), BF16),
            pltpu.VMEM((NY, 128, 128), BF16),
            pltpu.VMEM((NY, 128, 128), BF16),
            pltpu.VMEM((8, 256, 128), BF16),
            pltpu.VMEM((PARTS, 32, 128), BF16),
            pltpu.VMEM((CUBE, 32, 128), BF16),
            pltpu.VMEM((4, 32, 128), BF16),
            pltpu.VMEM((PARTS, 32, 128), BF16),
            pltpu.VMEM((10, 16, 128), BF16),
            pltpu.VMEM((8, 64, 128), F32),
            pltpu.VMEM((HEADS, 64, 128), BF16),
            dma((8,)),
            dma, dma((NY - 1,)),
            dma, dma,
            dma, dma, dma,
            dma, dma((NY,)), dma,
            dma, dma, dma, dma, dma, dma, dma, dma,
        ],
        compiler_params=pltpu.CompilerParams(
            collective_id=0, has_side_effects=True, vmem_limit_bytes=56 * 2**20
        ),
        name="graph_layer",
    )(
        node_feats, norm_gain.reshape(1, -1), w_qkv.T, rand_feat[0], temper.reshape(1, 1), edge_src,
        edge_count, block_fill,
    )
    return lax.dot_general(
        back.reshape(512, 128), w_out, (((0,), (0,)), ((), ())), preferred_element_type=F32
    ).astype(BF16)


def solution(mesh):
    return jax.shard_map(
        shards,
        mesh=mesh,
        in_specs=(
            P(("dom", "head"), None),
            P(),
            P(None, "head"),
            P(),
            P("head", None, None),
            P("head"),
            P("dom", None),
            P("dom"),
            P(),
        ),
        out_specs=P(("dom", "head"), None),
        check_vma=False,
    )
```
